512 devices in a mesh: runs: 64 (over y, x, core), cells: 8 (over z).
Axes of the slice: x: 4, y: 8, z: 8, core: 2. Of those that a mesh axis runs over, the one named last changes fastest.
Arguments:
- maps: bfloat16 [8192, 16384], P('runs', 'cells'), may hold values from -6 to 6
- run_inputs: bfloat16 [8, 8192], P(None, 'runs'), may hold values from 0 to 1
- basis: bfloat16 [16384, 256], P('cells'), may hold values from -0.375 to 0.375
- amplitude: float32 [8], replicated, may hold values from 0.02 to 0.045
- length: float32 [8, 8], replicated, may hold values from 0.27 to 0.33
- noise: float32 [8192], P('runs'), may hold values from 0.1 to 0.2
Outputs:
- product: bfloat16 [8192, 16384], P('runs', 'cells')
The draws below stay inside these ranges and needn't reach their ends.
All inputs are finite; a program needn't handle non-finite values.
Results may differ from the reference program's by a relative error of at most 0.0064.
Values may be sent and summed in bfloat16 or wider, within the bound.
A program may use at most 64 MiB of HBM per device.

```python
import math
import jax
import jax.numpy as jnp
from jax import lax

CELLS = 16384
LAT = 8
RANK = 32
DIN = 8
RUNS = 8192


def draw_run_inputs(key, part):
    key = jax.random.fold_in(key, 11)
    values = jax.random.uniform(key, (DIN, RUNS), jnp.float32, 0.0, 1.0)
    return values.astype(jnp.bfloat16)


def levels(key, shape, split, smallest, largest):
    factor_of = 1.0
    for position, parts in split:
        draws = jax.random.uniform(jax.random.fold_in(jax.random.fold_in(key, 6), position), (parts,), jnp.float32, smallest / len(split), largest / len(split))
        factor_of = factor_of * jnp.repeat(jnp.exp(draws), shape[position] // parts).reshape((-1,) + (1,) * (len(shape) - 1 - position))
    return factor_of


def bell_draw(stream_key, dims, scale, limit, shards=(), held_as=jnp.bfloat16):
    values = jax.random.normal(stream_key, dims, jnp.float32) * scale
    if len(shards) > 0:
        values = levels(stream_key, dims, shards, -0.22, 0.18) * values
    return jnp.clip(values, min=-limit, max=limit).astype(held_as)


def setup_inputs(seed: int = 0) -> dict:
    key_of = jax.random.split(jax.random.key(seed), 7)
    return {
        "maps": bell_draw(key_of[0], (RUNS, CELLS), 1.0, 6.0, ((0, 64), (1, 8))),
        "run_inputs": draw_run_inputs(jax.random.fold_in(key_of[6], 71), 0),
        "basis": bell_draw(key_of[2], (CELLS, LAT * RANK), (LAT * RANK) ** -0.5, 0.375, ((0, 8),)),
        "amplitude": jnp.clip(jnp.exp(jax.random.uniform(key_of[3], (LAT,), jnp.float32, math.log(0.02), math.log(0.045))), 0.02, 0.045),
        "length": jnp.clip(jnp.exp(jax.random.uniform(key_of[4], (LAT, DIN), jnp.float32, math.log(0.27), math.log(0.33))), 0.27, 0.33),
        "noise": jnp.clip(jnp.exp(math.log(0.2) - 0.6931472 * jax.random.uniform(key_of[5], (RUNS,), jnp.float32) ** levels(key_of[5], (RUNS,), ((0, 64),), -0.2, 0.2)), 0.1, 0.2),
    }


def reference(maps, run_inputs, basis, amplitude, length, noise):
    lat = amplitude.shape[0]
    rank = basis.shape[1] // lat
    projected = jnp.dot(maps, basis, preferred_element_type=jnp.float32).astype(jnp.bfloat16)
    inverse = 1.0 / length
    scaled = run_inputs.astype(jnp.float32)[None, :, :] * inverse[:, :, None]
    half = 0.5 * jnp.sum(scaled * scaled, axis=1)
    proj_wide = projected.astype(jnp.float32).reshape(RUNS, lat, rank)
    block = math.gcd(RUNS, 512)
    count = RUNS // block

    def row_block(index):
        start = (index * block).astype(jnp.int32)
        rows_scaled = lax.dynamic_slice_in_dim(scaled, start, block, 2)
        rows_half = lax.dynamic_slice_in_dim(half, start, block, 1)
        logit = jnp.einsum("qdr,qdc->qrc", rows_scaled, scaled, precision=lax.Precision.HIGHEST)
        logit = logit - rows_half[:, :, None] - half[:, None, :]
        tile = (amplitude[:, None, None] * jnp.exp(jnp.minimum(logit, 0.0))).astype(jnp.bfloat16)
        values = jnp.einsum("qrc,cqk->rqk", tile.astype(jnp.float32), proj_wide, precision=lax.Precision.HIGHEST)
        return values.reshape(block, lat * rank)

    latent = lax.map(row_block, jnp.arange(count, dtype=jnp.int32))
    latent = latent.reshape(RUNS, lat * rank).astype(jnp.bfloat16)
    expand = jnp.dot(latent, basis.T, preferred_element_type=jnp.float32)
    return (expand + noise[:, None] * maps.astype(jnp.float32)).astype(jnp.bfloat16)
```

```python
import jax
import jax.numpy as jnp
from jax import lax
from jax.experimental import pallas as pl
from jax.experimental.pallas import tpu as pltpu
from jax.sharding import PartitionSpec as P

MESH = pl.DeviceIdType.MESH
F32 = jnp.float32
BF16 = jnp.bfloat16
NY, NX, NC, NZ = 8, 4, 2, 8
NJ = NX * NC
ROWS = 128
RANK = 32
DIN = 8
CELLS = 2048
WIDTH = NZ * RANK
LOADS = 4
STEP = CELLS // LOADS


def split3(value):
    high = value.astype(BF16).astype(F32)
    rest = value - high
    mid = rest.astype(BF16).astype(F32)
    return high, mid, rest - mid


def pick(index, *values):
    out = jnp.zeros((8, ROWS), F32)
    for place, value in enumerate(values):
        out = jnp.where(index == place, value, out)
    return out


def kernel(
    x_ref, amp_ref, len_ref, noise_ref, maps_hbm, basis_hbm, out_hbm,
    maps, basis, outs, rows_x, cols_x, part_wide, part, part_in, proj, tile, side,
    sums, sums_in, latent, load_sem, store_sem, send_sem, recv_sem,
):
    run = lax.axis_index("runs")
    z = lax.axis_index("cells")
    y, j = run // NJ, run % NJ
    x, core = j // NC, j % NC

    def along_z(step):
        return (run, (z + step + NZ) % NZ)

    def along_y(step):
        return (((y + step + NY) % NY) * NJ + j, z)

    def along_j(slot, sign=1):
        dx, dc = slot // NC, slot % NC
        return (y * NJ + ((x + sign * dx + NX) % NX) * NC + (core + dc) % NC, z)

    barrier = pltpu.get_barrier_semaphore()
    for step in range(1, 8):
        for device in (along_z(step), along_y(step), along_j(step)):
            pl.semaphore_signal(barrier, inc=1, device_id=device, device_id_type=MESH)

    loads = []
    for c in range(LOADS):
        now = pl.ds(c * STEP, STEP)
        loads.append((
            pltpu.make_async_copy(maps_hbm.at[:, now], maps.at[:, now], load_sem.at[0, c]),
            pltpu.make_async_copy(basis_hbm.at[now], basis.at[now], load_sem.at[1, c]),
        ))
        for load in loads[-1]:
            load.start()

    def remote(phase, slot, source, target, device):
        return pltpu.make_async_remote_copy(
            src_ref=source, dst_ref=target, send_sem=send_sem.at[phase, slot],
            recv_sem=recv_sem.at[phase, slot], device_id=device, device_id_type=MESH,
        )

    mine = x_ref[...].astype(F32)
    rows_x[0] = mine
    cols_x[0] = mine
    pl.semaphore_wait(barrier, 21)

    sent = []
    rows_in = {}
    cols_in = {}
    for slot in range(1, 8):
        rows_in[slot] = remote(0, slot, rows_x.at[0], rows_x.at[slot], along_y(slot))
        cols_in[slot] = remote(1, slot, cols_x.at[0], cols_x.at[slot], along_j(slot))
        rows_in[slot].start()
        cols_in[slot].start()

    total = jnp.zeros((ROWS, WIDTH), F32)
    for c in range(LOADS):
        for load in loads[c]:
            load.wait()
        now = pl.ds(c * STEP, STEP)
        total = total + jnp.dot(maps[:, now], basis[now, :], preferred_element_type=F32)
    turned = total.T.reshape(NZ, RANK, ROWS)
    part_wide[...] = turned
    part[...] = turned.astype(BF16)
    part_sends = {}
    for slot in (4, 3, 5, 2, 6, 1, 7):
        peer = along_z(slot)
        part_sends[slot] = remote(2, slot, part.at[peer[1]], part_in.at[slot], peer)
        part_sends[slot].start()

    index = lax.broadcasted_iota(jnp.int32, (8, ROWS), 0)
    length = len_ref[pl.ds(z, 1), :]
    square = (DIN, DIN)
    eye = lax.broadcasted_iota(jnp.int32, square, 0) == lax.broadcasted_iota(jnp.int32, square, 1)
    column = jnp.sum(jnp.where(eye, jnp.broadcast_to(length, square), 0.0), axis=1, keepdims=True)
    inverse = 1.0 / column
    squared = inverse * inverse
    amp = amp_ref[z]

    def halves(inputs):
        scaled = inputs * inverse
        return split3(0.5 * jnp.sum(scaled * scaled, axis=0, keepdims=True))

    for slot in range(1, 8):
        rows_in[slot].wait_recv()
    for slot in range(NY):
        inputs = rows_x[slot]
        ha, hb, hc = halves(inputs)
        wa, wb, wc = split3(inputs * squared)
        tail = pick(index, -ha, -hb, -hc, -1.0, -1.0, -1.0)
        side[:, slot * ROWS:(slot + 1) * ROWS] = jnp.concatenate([wa, wb, wc, tail], 0).astype(BF16)
    for slot in range(1, 8):
        cols_in[slot].wait_recv()

    @pl.loop(0, NJ)
    def _(slot):
        inputs = cols_x[slot]
        ha, hb, hc = halves(inputs)
        tail = pick(index, 1.0, 1.0, 1.0, ha, hb, hc)
        left = jnp.concatenate([inputs, inputs, inputs, tail], 0).T.astype(BF16)
        logit = jnp.dot(left, side[...], preferred_element_type=F32)
        tile[slot] = (amp * jnp.exp(jnp.minimum(logit, 0.0))).astype(BF16)

    own = part_wide[z]
    for slot in range(1, 8):
        part_sends[slot].wait_recv()
        own = own + part_in[slot].astype(F32)
    proj[0] = own.astype(BF16)
    proj_sends = {}
    for slot in (4, 5, 2, 3, 6, 7, 1):
        proj_sends[slot] = remote(3, slot, proj.at[0], proj.at[slot], along_j(slot))
        proj_sends[slot].start()

    values = jnp.zeros((RANK, NY * ROWS), F32)
    for pair in (0, 1, 3, 2):
        for slot in (2 * pair, 2 * pair + 1):
            if slot:
                proj_sends[slot].wait_recv()
        block = jnp.concatenate([proj[2 * pair], proj[2 * pair + 1]], 1)
        weights = tile[2 * pair:2 * pair + 2].reshape(2 * ROWS, NY * ROWS)
        values = values + jnp.dot(block, weights, preferred_element_type=F32)

    sum_sends = {}
    for slot in (4, 3, 5, 2, 6, 1, 7):
        sums[slot] = values[:, slot * ROWS:(slot + 1) * ROWS].astype(BF16)
        sum_sends[slot] = remote(4, slot, sums.at[slot], sums_in.at[slot], along_y(-slot))
        sum_sends[slot].start()
    final = values[:, :ROWS]
    for slot in range(1, 8):
        sum_sends[slot].wait_recv()
        final = final + sums_in[slot].astype(F32)
    latent[z] = final.astype(BF16)
    latent_sends = {}
    for slot in (4, 3, 5, 2, 6, 1, 7):
        latent_sends[slot] = remote(5, slot, latent.at[z], latent.at[z], along_z(slot))
        latent_sends[slot].start()

    whole = (ROWS, ROWS)
    eye = lax.broadcasted_iota(jnp.int32, whole, 0) == lax.broadcasted_iota(jnp.int32, whole, 1)
    spread = jnp.where(eye, jnp.broadcast_to(noise_ref[...], whole), 0.0)
    noise = jnp.sum(spread, axis=1, keepdims=True)

    for slot in range(1, 8):
        latent_sends[slot].wait_recv()
    mixed = latent[...].reshape(WIDTH, ROWS).astype(F32).T.astype(BF16)
    stores = []
    for c in range(LOADS):
        now = pl.ds(c * STEP, STEP)
        expand = lax.dot_general(
            mixed, basis[now, :], (((1,), (1,)), ((), ())), preferred_element_type=F32
        )
        outs[:, now] = (expand + noise * maps[:, now].astype(F32)).astype(BF16)
        stores.append(pltpu.make_async_copy(outs.at[:, now], out_hbm.at[:, now], store_sem.at[c]))
        stores[-1].start()

    for group in (rows_in, cols_in, part_sends, proj_sends, sum_sends, latent_sends):
        for slot in range(1, 8):
            group[slot].wait_send()
    for store in stores:
        store.wait()


def shards(maps, run_inputs, basis, amplitude, length, noise):
    vmem = pl.BlockSpec(memory_space=pltpu.VMEM)
    smem = pl.BlockSpec(memory_space=pltpu.SMEM)
    hbm = pl.BlockSpec(memory_space=pl.ANY)
    block = (8, RANK, ROWS)
    return pl.pallas_call(
        kernel,
        out_shape=jax.ShapeDtypeStruct((ROWS, CELLS), BF16),
        in_specs=[vmem, smem, vmem, vmem, hbm, hbm],
        out_specs=hbm,
        scratch_shapes=[
            pltpu.VMEM((ROWS, CELLS), BF16),
            pltpu.VMEM((CELLS, WIDTH), BF16),
            pltpu.VMEM((ROWS, CELLS), BF16),
            pltpu.VMEM((NY, DIN, ROWS), F32),
            pltpu.VMEM((NJ, DIN, ROWS), F32),
            pltpu.VMEM(block, F32),
            pltpu.VMEM(block, BF16),
            pltpu.VMEM(block, BF16),
            pltpu.VMEM(block, BF16),
            pltpu.VMEM((NJ, ROWS, NY * ROWS), BF16),
            pltpu.VMEM((RANK, NY * ROWS), BF16),
            pltpu.VMEM(block, BF16),
            pltpu.VMEM(block, BF16),
            pltpu.VMEM(block, BF16),
            pltpu.SemaphoreType.DMA((2, LOADS)),
            pltpu.SemaphoreType.DMA((LOADS,)),
            pltpu.SemaphoreType.DMA((6, 8)),
            pltpu.SemaphoreType.DMA((6, 8)),
        ],
        compiler_params=pltpu.CompilerParams(
            collective_id=0, has_side_effects=True, vmem_limit_bytes=32 * 1024 * 1024
        ),
    )(run_inputs, amplitude, length, noise.reshape(1, ROWS), maps, basis)


def solution(mesh):
    in_specs = (P("runs", "cells"), P(None, "runs"), P("cells", None), P(), P(), P("runs"))
    out_specs = P("runs", "cells")
    return jax.shard_map(shards, mesh=mesh, in_specs=in_specs, out_specs=out_specs, check_vma=False)
```

```python
import jax
import jax.numpy as jnp
from jax import lax
from jax.experimental import pallas as pl
from jax.experimental.pallas import tpu as pltpu
from jax.sharding import PartitionSpec as P

MESH = pl.DeviceIdType.MESH
F32 = jnp.float32
BF16 = jnp.bfloat16
NY, NX, NC, NZ = 8, 4, 2, 8
ROWS = 128
PAIR = NC * ROWS
RANK = 32
DIN = 8
CELLS = 2048
WIDTH = NZ * RANK
LOADS = 4
STEP = CELLS // LOADS
FAR = (4, 3, 5, 2, 6, 1, 7)
ROW, COL, PART, PROJ, SUM, LAT0, LAT1 = range(7)


def split3(value):
    high = value.astype(BF16).astype(F32)
    rest = value - high
    mid = rest.astype(BF16).astype(F32)
    return high, mid, rest - mid


def pick(index, *values):
    out = jnp.zeros(index.shape, F32)
    for place, value in enumerate(values):
        out = jnp.where(index == place, value, out)
    return out


def kernel(
    x_hbm, amp_hbm, len_hbm, noise_hbm, maps_hbm, basis_hbm, out_ref,
    x_ref, amp_ref, len_ref, noise_ref, maps, basis, basis_t, base, mine, rows_x, cols_x,
    part_wide, part, part_in, proj, left, side, tile, sums, sums_in, lat_src, latent,
    load_sem, send_sem, recv_sem,
):
    run = lax.axis_index("runs")
    z = lax.axis_index("cells")
    y, x, core = run // (NX * NC), (run // NC) % NX, run % NC
    owner = core == 1

    def at(dy, dx, to, dz):
        place = ((y + dy + NY) % NY) * (NX * NC) + ((x + dx + NX) % NX) * NC + to
        return (place, (z + dz + NZ) % NZ)

    loads = []
    for c in range(LOADS):
        now = pl.ds(c * STEP, STEP)
        loads.append((
            pltpu.make_async_copy(maps_hbm.at[:, now], maps.at[:, now], load_sem.at[0, c]),
            pltpu.make_async_copy(basis_hbm.at[now], basis.at[now], load_sem.at[1, c]),
        ))
    small = [
        pltpu.make_async_copy(source, target, load_sem.at[2, place])
        for place, (source, target) in enumerate(
            ((x_hbm, x_ref), (len_hbm, len_ref), (amp_hbm, amp_ref), (noise_hbm, noise_ref))
        )
    ]
    for load in (*small, *loads[0], *loads[1], *loads[2], *loads[3]):
        load.start()

    barrier = pltpu.get_barrier_semaphore()

    def greet(device):
        pl.semaphore_signal(barrier, inc=1, device_id=device, device_id_type=MESH)

    @pl.when(owner)
    def _():
        for d in FAR:
            for to in range(NC):
                greet(at(d, 0, to, 0))
                greet(at(0, 0, to, d))
        for d in (2, 1, 3):
            for to in range(NC):
                greet(at(0, d, to, 0))
        greet(at(0, 0, 0, 0))

    @pl.when(jnp.logical_not(owner))
    def _():
        for d in (*FAR, 0):
            greet(at(0, 0, 1, d))

    def remote(phase, slot, source, target, device, to=0):
        return pltpu.make_async_remote_copy(
            src_ref=source, dst_ref=target, send_sem=send_sem.at[phase, slot],
            recv_sem=recv_sem.at[phase, slot, to], device_id=device, device_id_type=MESH,
        )

    def send_row(d):
        return remote(ROW, d, mine, rows_x.at[d, core], at(d, 0, 1, 0), core)

    def send_col(d):
        return remote(COL, d, mine, cols_x.at[d, core], at(0, d, 1, 0), core)

    def send_part(d):
        return remote(PART, d, part.at[(z + d) % NZ], part_in.at[d, core], at(0, 0, 1, d), core)

    def send_proj(d):
        return remote(PROJ, d, proj.at[0], proj.at[d], at(0, d, 1, 0))

    def send_sum(d):
        return remote(SUM, d, sums.at[d], sums_in.at[d], at(-d, 0, 1, 0))

    def send_latent(d, to):
        return remote(LAT0 + to, d, lat_src.at[to], latent.at[z], at(0, 0, to, d))

    def got(phase, slot, to, target):
        pltpu.make_async_remote_copy(
            src_ref=target, dst_ref=target, send_sem=send_sem.at[phase, slot],
            recv_sem=recv_sem.at[phase, slot, to], device_id=at(0, 0, 1, 1), device_id_type=MESH,
        ).wait_recv()

    for load in small:
        load.wait()
    mine[...] = x_ref[...].astype(F32)

    @pl.when(owner)
    def _():
        pl.semaphore_wait(barrier, 25)
        rows_x[0, 1] = mine[...]

    @pl.when(jnp.logical_not(owner))
    def _():
        pl.semaphore_wait(barrier, 18)
        send_row(0).start()

    for d in FAR:
        send_row(d).start()
    for d in (2, 1, 3):
        send_col(d).start()

    total = jnp.zeros((ROWS, WIDTH), F32)
    for c in range(LOADS):
        for load in loads[c]:
            load.wait()
        now = pl.ds(c * STEP, STEP)
        total = total + jnp.dot(maps[:, now], basis[now, :], preferred_element_type=F32)
    turned = total.T.reshape(NZ, RANK, ROWS)
    part_wide[...] = turned
    part[...] = turned.astype(BF16)
    for d in FAR:
        send_part(d).start()

    @pl.when(jnp.logical_not(owner))
    def _():
        send_part(0).start()

    whole = (ROWS, ROWS)
    eye = lax.broadcasted_iota(jnp.int32, whole, 0) == lax.broadcasted_iota(jnp.int32, whole, 1)
    spread = jnp.where(eye, jnp.broadcast_to(noise_ref[...], whole), 0.0)
    noise = jnp.sum(spread, axis=1, keepdims=True)

    @pl.loop(0, CELLS // PAIR)
    def _(c):
        now = pl.ds(pl.multiple_of(c * PAIR, PAIR), PAIR)
        base[:, now] = noise * maps[:, now].astype(F32)
        basis_t[:, now] = basis[now, :].T

    @pl.when(owner)
    def _():
        length = len_ref[pl.ds(z, 1), :]
        square = (DIN, DIN)
        eye = lax.broadcasted_iota(jnp.int32, square, 0) == lax.broadcasted_iota(jnp.int32, square, 1)
        column = jnp.sum(jnp.where(eye, jnp.broadcast_to(length, square), 0.0), axis=1, keepdims=True)
        inverse = 1.0 / column
        squared = inverse * inverse
        lanes = lax.broadcasted_iota(jnp.int32, (1, NZ), 1)
        amp = jnp.sum(jnp.where(lanes == z, amp_ref[...], 0.0), axis=1, keepdims=True)
        index = lax.broadcasted_iota(jnp.int32, (DIN, PAIR), 0)

        def halves(inputs):
            scaled = inputs * inverse
            return split3(0.5 * jnp.sum(scaled * scaled, axis=0, keepdims=True))

        def both(ref, slot):
            return jnp.concatenate([ref[slot, 0], ref[slot, 1]], 1)

        for d in range(NY):
            for to in range(NC):
                if d or not to:
                    got(ROW, d, to, rows_x.at[d, to])
        cols_x[0] = rows_x[0]
        for d in range(NY):
            inputs = both(rows_x, d)
            ha, hb, hc = halves(inputs)
            wa, wb, wc = split3(inputs * squared)
            tail = pick(index, -ha, -hb, -hc, -1.0, -1.0, -1.0)
            side[:, d * PAIR:(d + 1) * PAIR] = jnp.concatenate([wa, wb, wc, tail], 0).astype(BF16)
        for d in range(NX):
            if d:
                for to in range(NC):
                    got(COL, d, to, cols_x.at[d, to])
            inputs = both(cols_x, d)
            ha, hb, hc = halves(inputs)
            tail = pick(index, 1.0, 1.0, 1.0, ha, hb, hc)
            left[d] = jnp.concatenate([inputs, inputs, inputs, tail], 0).T.astype(BF16)

        own = [jnp.zeros((RANK, ROWS), F32), part_wide[z]]
        for d in (0, 1, 7, 2, 6, 3, 5, 4):
            for to in range(NC):
                if d or not to:
                    got(PART, d, to, part_in.at[d, to])
                    own[to] = own[to] + part_in[d, to].astype(F32)
        for to in range(NC):
            proj[0, to] = own[to].astype(BF16)
        for d in (2, 1, 3):
            send_proj(d).start()

        @pl.loop(0, NX * NC)
        def _(step):
            d, half = step // NC, step % NC
            now = pl.ds(pl.multiple_of(half * (NY * ROWS), NY * ROWS), NY * ROWS)
            logit = jnp.dot(left[d], side[:, now], preferred_element_type=F32)
            tile[d, :, now] = (amp * jnp.exp(jnp.minimum(logit, 0.0))).astype(BF16)

        for d in (1, 3, 2):
            got(PROJ, d, 0, proj.at[d])
        blocks = [both(proj, d) for d in range(NX)]
        for d in (*FAR, 0):
            now = pl.ds(d * PAIR, PAIR)
            values = jnp.zeros((RANK, PAIR), F32)
            for e in range(NX):
                values = values + jnp.dot(blocks[e], tile[e, :, now], preferred_element_type=F32)
            if d:
                sums[d, 0] = values[:, :ROWS].astype(BF16)
                sums[d, 1] = values[:, ROWS:].astype(BF16)
                send_sum(d).start()
        final = [values[:, :ROWS], values[:, ROWS:]]
        for d in (1, 7, 2, 6, 3, 5, 4):
            got(SUM, d, 0, sums_in.at[d])
            for to in range(NC):
                final[to] = final[to] + sums_in[d, to].astype(F32)
        for to in range(NC):
            lat_src[to] = final[to].astype(BF16)
        latent[z] = final[1].astype(BF16)
        for d in FAR:
            send_latent(d, 0).start()
            send_latent(d, 1).start()
        send_latent(0, 0).start()

        for d in (1, 7, 2, 6, 3, 5, 4):
            got(LAT1, d, 0, latent.at[(z + NZ - d) % NZ])

    @pl.when(jnp.logical_not(owner))
    def _():
        for d in (0, 1, 7, 2, 6, 3, 5, 4):
            got(LAT0, d, 0, latent.at[(z + NZ - d) % NZ])

    mixed = latent[...].reshape(WIDTH, ROWS).astype(F32).T.astype(BF16)
    for c in range(LOADS):
        now = pl.ds(c * STEP, STEP)
        expand = jnp.dot(mixed, basis_t[:, now], preferred_element_type=F32)
        out_ref[:, now] = (expand + base[:, now]).astype(BF16)

    for d in FAR:
        send_row(d).wait_send()
        send_part(d).wait_send()
    for d in (1, 2, 3):
        send_col(d).wait_send()

    @pl.when(owner)
    def _():
        for d in (1, 2, 3):
            send_proj(d).wait_send()
        for d in FAR:
            send_sum(d).wait_send()
            send_latent(d, 1).wait_send()
            send_latent(d, 0).wait_send()
        send_latent(0, 0).wait_send()

    @pl.when(jnp.logical_not(owner))
    def _():
        send_row(0).wait_send()
        send_part(0).wait_send()


def shards(maps, run_inputs, basis, amplitude, length, noise):
    operands = (run_inputs, amplitude.reshape(1, NZ), length, noise.reshape(1, ROWS), maps, basis)
    operands = [pltpu.with_memory_space_constraint(a, pltpu.HBM) for a in operands]
    hbm = pl.BlockSpec(memory_space=pltpu.HBM)
    return pl.pallas_call(
        kernel,
        out_shape=pltpu.VMEM((ROWS, CELLS), BF16),
        in_specs=[hbm] * 6,
        out_specs=pl.BlockSpec(memory_space=pltpu.VMEM),
        scratch_shapes=[
            pltpu.VMEM((DIN, ROWS), BF16),
            pltpu.VMEM((1, NZ), F32),
            pltpu.VMEM((NZ, DIN), F32),
            pltpu.VMEM((1, ROWS), F32),
            pltpu.VMEM((ROWS, CELLS), BF16),
            pltpu.VMEM((CELLS, WIDTH), BF16),
            pltpu.VMEM((WIDTH, CELLS), BF16),
            pltpu.VMEM((ROWS, CELLS), F32),
            pltpu.VMEM((DIN, ROWS), F32),
            pltpu.VMEM((NY, NC, DIN, ROWS), F32),
            pltpu.VMEM((NX, NC, DIN, ROWS), F32),
            pltpu.VMEM((NZ, RANK, ROWS), F32),
            pltpu.VMEM((NZ, RANK, ROWS), BF16),
            pltpu.VMEM((NZ, NC, RANK, ROWS), BF16),
            pltpu.VMEM((NX, NC, RANK, ROWS), BF16),
            pltpu.VMEM((NX, PAIR, RANK), BF16),
            pltpu.VMEM((RANK, NY * PAIR), BF16),
            pltpu.VMEM((NX, PAIR, NY * PAIR), BF16),
            pltpu.VMEM((NY, NC, RANK, ROWS), BF16),
            pltpu.VMEM((NY, NC, RANK, ROWS), BF16),
            pltpu.VMEM((NC, RANK, ROWS), BF16),
            pltpu.VMEM((NZ, RANK, ROWS), BF16),
            pltpu.SemaphoreType.DMA((3, LOADS)),
            pltpu.SemaphoreType.DMA((7, 8)),
            pltpu.SemaphoreType.DMA((7, 8, NC)),
        ],
        compiler_params=pltpu.CompilerParams(
            collective_id=0, has_side_effects=True, vmem_limit_bytes=32 * 1024 * 1024
        ),
    )(*operands)


def solution(mesh):
    in_specs = (P("runs", "cells"), P(None, "runs"), P("cells", None), P(), P(), P("runs"))
    out_specs = P("runs", "cells")
    return jax.shard_map(shards, mesh=mesh, in_specs=in_specs, out_specs=out_specs, check_vma=False)
```

```python
import jax
import jax.numpy as jnp
from jax import lax
from jax.experimental import pallas as pl
from jax.experimental.pallas import tpu as pltpu
from jax.sharding import PartitionSpec as P

MESH = pl.DeviceIdType.MESH
F32 = jnp.float32
BF16 = jnp.bfloat16
NY, NX, NC, NZ = 8, 4, 2, 8
ROWS = 128
PAIR = NC * ROWS
RANK = 32
DIN = 8
CELLS = 2048
WIDTH = NZ * RANK
LOADS = 4
STEP = CELLS // LOADS
FAR = (4, 3, 5, 2, 6, 1, 7)
ROW, COL, PART, PROJ, SUM, LAT0, LAT1 = range(7)


def split3(value):
    high = value.astype(BF16).astype(F32)
    rest = value - high
    mid = rest.astype(BF16).astype(F32)
    return high, mid, rest - mid


def pick(index, *values):
    out = jnp.zeros(index.shape, F32)
    for place, value in enumerate(values):
        out = jnp.where(index == place, value, out)
    return out


def kernel(
    x_hbm, amp_hbm, len_hbm, noise_hbm, maps_hbm, basis_hbm, out_ref,
    x_ref, amp_ref, len_ref, noise_ref, maps, basis, basis_t, base, mine, rows_x, cols_x,
    part_wide, part, part_in, proj, left, side, tile, sums, sums_in, lat_src, latent,
    load_sem, send_sem, recv_sem,
):
    run = lax.axis_index("runs")
    z = lax.axis_index("cells")
    y, x, core = run // (NX * NC), (run // NC) % NX, run % NC
    owner = core == 1

    def at(dy, dx, to, dz):
        place = ((y + dy + NY) % NY) * (NX * NC) + ((x + dx + NX) % NX) * NC + to
        return (place, (z + dz + NZ) % NZ)

    barrier = pltpu.get_barrier_semaphore()

    def greet(device):
        pl.semaphore_signal(barrier, inc=1, device_id=device, device_id_type=MESH)

    @pl.when(owner)
    def _():
        for d in FAR:
            for to in range(NC):
                greet(at(0, 0, to, d))

    @pl.when(jnp.logical_not(owner))
    def _():
        for d in (*FAR, 0):
            greet(at(0, 0, 1, d))

    loads = []
    for c in range(LOADS):
        now = pl.ds(c * STEP, STEP)
        loads.append((
            pltpu.make_async_copy(maps_hbm.at[:, now], maps.at[:, now], load_sem.at[0, c]),
            pltpu.make_async_copy(basis_hbm.at[now], basis.at[now], load_sem.at[1, c]),
        ))
    small = [
        pltpu.make_async_copy(source, target, load_sem.at[2, place])
        for place, (source, target) in enumerate(
            ((x_hbm, x_ref), (len_hbm, len_ref), (amp_hbm, amp_ref), (noise_hbm, noise_ref))
        )
    ]
    for load in (*loads[0], *loads[1], *loads[2], *loads[3], *small):
        load.start()

    @pl.when(owner)
    def _():
        for d in FAR:
            for to in range(NC):
                greet(at(d, 0, to, 0))
        for d in (2, 1, 3):
            for to in range(NC):
                greet(at(0, d, to, 0))
        greet(at(0, 0, 0, 0))

    def remote(phase, source, target, device):
        return pltpu.make_async_remote_copy(
            src_ref=source, dst_ref=target, send_sem=send_sem.at[phase],
            recv_sem=recv_sem.at[phase], device_id=device, device_id_type=MESH,
        )

    def received(phase, target):
        remote(phase, target, target, at(0, 0, 1, 1)).wait_recv()

    def left_here(phase, source):
        remote(phase, source, source, at(0, 0, 1, 1)).wait_send()

    def send_row(d):
        remote(ROW, mine, rows_x.at[d * NC + core], at(d, 0, 1, 0)).start()

    def send_part(d):
        remote(PART, part.at[(z + d) % NZ], part_in.at[d * NC + core], at(0, 0, 1, d)).start()

    total = jnp.zeros((ROWS, WIDTH), F32)
    for c in range(LOADS):
        for load in loads[c]:
            load.wait()
        now = pl.ds(c * STEP, STEP)
        total = total + jnp.dot(maps[:, now], basis[now, :], preferred_element_type=F32)
    turned = total.T.reshape(NZ, RANK, ROWS)
    part_wide[...] = turned
    part[...] = turned.astype(BF16)
    for load in small:
        load.wait()
    mine[...] = x_ref[...].astype(F32)

    @pl.when(owner)
    def _():
        pl.semaphore_wait(barrier, 25)

    @pl.when(jnp.logical_not(owner))
    def _():
        pl.semaphore_wait(barrier, 18)

    for d in FAR:
        send_part(d)
    for d in FAR:
        send_row(d)
    for d in (2, 1, 3):
        remote(COL, mine, cols_x.at[d * NC + core], at(0, d, 1, 0)).start()

    @pl.when(jnp.logical_not(owner))
    def _():
        send_part(0)
        send_row(0)

    whole = (ROWS, ROWS)
    eye = lax.broadcasted_iota(jnp.int32, whole, 0) == lax.broadcasted_iota(jnp.int32, whole, 1)
    spread = jnp.where(eye, jnp.broadcast_to(noise_ref[...], whole), 0.0)
    noise = jnp.sum(spread, axis=1, keepdims=True)

    @pl.loop(0, CELLS // PAIR)
    def _(c):
        now = pl.ds(pl.multiple_of(c * PAIR, PAIR), PAIR)
        base[:, now] = noise * maps[:, now].astype(F32)
        basis_t[:, now] = basis[now, :].T

    @pl.when(owner)
    def _():
        length = len_ref[pl.ds(z, 1), :]
        square = (DIN, DIN)
        eye = lax.broadcasted_iota(jnp.int32, square, 0) == lax.broadcasted_iota(jnp.int32, square, 1)
        column = jnp.sum(jnp.where(eye, jnp.broadcast_to(length, square), 0.0), axis=1, keepdims=True)
        inverse = 1.0 / column
        squared = inverse * inverse
        lanes = lax.broadcasted_iota(jnp.int32, (1, NZ), 1)
        amp = jnp.sum(jnp.where(lanes == z, amp_ref[...], 0.0), axis=1, keepdims=True)

        def halves(inputs):
            scaled = inputs * inverse
            return split3(0.5 * jnp.sum(scaled * scaled, axis=0, keepdims=True))

        def side_by_side(ref, count):
            return jnp.concatenate([ref[k] for k in range(count)], 1)

        def place(count):
            return lax.broadcasted_iota(jnp.int32, (DIN, count), 0)

        received(PART, part_in.at[pl.ds(0, NZ * NC - 1)])
        own = [part_in[0].astype(F32), part_wide[z]]
        for d in range(1, NZ):
            for to in range(NC):
                own[to] = own[to] + part_in[d * NC + to].astype(F32)
        for to in range(NC):
            proj[0, to] = own[to].astype(BF16)
        for d in (2, 1, 3):
            remote(PROJ, proj.at[0], proj.at[d], at(0, d, 1, 0)).start()

        received(ROW, rows_x.at[pl.ds(0, NY * NC - 1)])
        rows_x[1] = mine[...]
        inputs = side_by_side(rows_x, NY * NC)
        ha, hb, hc = halves(inputs)
        wa, wb, wc = split3(inputs * squared)
        tail = pick(place(NY * PAIR), -ha, -hb, -hc, -1.0, -1.0, -1.0)
        side[...] = jnp.concatenate([wa, wb, wc, tail], 0).astype(BF16)
        received(COL, cols_x.at[pl.ds(0, (NX - 1) * NC)])
        for to in range(NC):
            cols_x[to] = rows_x[to]
        inputs = side_by_side(cols_x, NX * NC)
        ha, hb, hc = halves(inputs)
        tail = pick(place(NX * PAIR), 1.0, 1.0, 1.0, ha, hb, hc)
        left[...] = jnp.concatenate([inputs, inputs, inputs, tail], 0).T.astype(BF16)

        @pl.loop(0, NX)
        def _(d):
            now = pl.ds(pl.multiple_of(d * PAIR, PAIR), PAIR)
            logit = jnp.dot(left[now, :], side[...], preferred_element_type=F32)
            tile[d] = (amp * jnp.exp(jnp.minimum(logit, 0.0))).astype(BF16)

        received(PROJ, proj.at[pl.ds(1, NX - 1)])
        blocks = [jnp.concatenate([proj[d, 0], proj[d, 1]], 1) for d in range(NX)]
        for d in (*FAR, 0):
            now = pl.ds(d * PAIR, PAIR)
            values = jnp.zeros((RANK, PAIR), F32)
            for e in range(NX):
                values = values + jnp.dot(blocks[e], tile[e, :, now], preferred_element_type=F32)
            if d:
                sums[d, 0] = values[:, :ROWS].astype(BF16)
                sums[d, 1] = values[:, ROWS:].astype(BF16)
                remote(SUM, sums.at[d], sums_in.at[d], at(-d, 0, 1, 0)).start()
        received(SUM, sums_in.at[pl.ds(1, NY - 1)])
        final = [values[:, :ROWS], values[:, ROWS:]]
        for d in range(1, NY):
            for to in range(NC):
                final[to] = final[to] + sums_in[d, to].astype(F32)
        for to in range(NC):
            lat_src[to] = final[to].astype(BF16)
        for d in FAR:
            remote(LAT1, lat_src.at[1], latent.at[z], at(0, 0, 1, d)).start()
            remote(LAT0, lat_src.at[0], latent.at[z], at(0, 0, 0, d)).start()
        remote(LAT0, lat_src.at[0], latent.at[z], at(0, 0, 0, 0)).start()
        latent[z] = lat_src[1]

        left_here(ROW, rows_x.at[pl.ds(0, NY - 1)])
        left_here(COL, cols_x.at[pl.ds(0, NX - 1)])
        left_here(PART, part.at[pl.ds(0, NZ - 1)])
        left_here(PROJ, proj.at[pl.ds(0, NX - 1)])
        left_here(SUM, sums.at[pl.ds(0, NY - 1)])
        left_here(LAT0, part)
        left_here(LAT1, part.at[pl.ds(0, NZ - 1)])
        received(LAT1, latent.at[pl.ds(0, NZ - 1)])

    @pl.when(jnp.logical_not(owner))
    def _():
        left_here(ROW, rows_x.at[pl.ds(0, NY)])
        left_here(COL, cols_x.at[pl.ds(0, NX - 1)])
        left_here(PART, part)
        received(LAT0, latent)

    mixed = latent[...].reshape(WIDTH, ROWS).astype(F32).T.astype(BF16)
    for c in range(LOADS):
        now = pl.ds(c * STEP, STEP)
        expand = jnp.dot(mixed, basis_t[:, now], preferred_element_type=F32)
        out_ref[:, now] = (expand + base[:, now]).astype(BF16)


def shards(maps, run_inputs, basis, amplitude, length, noise):
    operands = (run_inputs, amplitude.reshape(1, NZ), length, noise.reshape(1, ROWS), maps, basis)
    operands = [pltpu.with_memory_space_constraint(a, pltpu.HBM) for a in operands]
    hbm = pl.BlockSpec(memory_space=pltpu.HBM)
    return pl.pallas_call(
        kernel,
        out_shape=pltpu.VMEM((ROWS, CELLS), BF16),
        in_specs=[hbm] * 6,
        out_specs=pl.BlockSpec(memory_space=pltpu.VMEM),
        scratch_shapes=[
            pltpu.VMEM((DIN, ROWS), BF16),
            pltpu.VMEM((1, NZ), F32),
            pltpu.VMEM((NZ, DIN), F32),
            pltpu.VMEM((1, ROWS), F32),
            pltpu.VMEM((ROWS, CELLS), BF16),
            pltpu.VMEM((CELLS, WIDTH), BF16),
            pltpu.VMEM((WIDTH, CELLS), BF16),
            pltpu.VMEM((ROWS, CELLS), F32),
            pltpu.VMEM((DIN, ROWS), F32),
            pltpu.VMEM((NY * NC, DIN, ROWS), F32),
            pltpu.VMEM((NX * NC, DIN, ROWS), F32),
            pltpu.VMEM((NZ, RANK, ROWS), F32),
            pltpu.VMEM((NZ, RANK, ROWS), BF16),
            pltpu.VMEM((NZ * NC, RANK, ROWS), BF16),
            pltpu.VMEM((NX, NC, RANK, ROWS), BF16),
            pltpu.VMEM((NX * PAIR, RANK), BF16),
            pltpu.VMEM((RANK, NY * PAIR), BF16),
            pltpu.VMEM((NX, PAIR, NY * PAIR), BF16),
            pltpu.VMEM((NY, NC, RANK, ROWS), BF16),
            pltpu.VMEM((NY, NC, RANK, ROWS), BF16),
            pltpu.VMEM((NC, RANK, ROWS), BF16),
            pltpu.VMEM((NZ, RANK, ROWS), BF16),
            pltpu.SemaphoreType.DMA((3, LOADS)),
            pltpu.SemaphoreType.DMA((7,)),
            pltpu.SemaphoreType.DMA((7,)),
        ],
        compiler_params=pltpu.CompilerParams(
            collective_id=0, has_side_effects=True, vmem_limit_bytes=32 * 1024 * 1024
        ),
    )(*operands)


def solution(mesh):
    in_specs = (P("runs", "cells"), P(None, "runs"), P("cells", None), P(), P(), P("runs"))
    out_specs = P("runs", "cells")
    return jax.shard_map(shards, mesh=mesh, in_specs=in_specs, out_specs=out_specs, check_vma=False)
```

```python
import jax
import jax.numpy as jnp
from jax import lax
from jax.experimental import pallas as pl
from jax.experimental.pallas import tpu as pltpu
from jax.sharding import PartitionSpec as P

MESH = pl.DeviceIdType.MESH
F32 = jnp.float32
BF16 = jnp.bfloat16
NY, NX, NC, NZ = 8, 4, 2, 8
ROWS = 128
HALF = NZ // 2
PAIR = NC * ROWS
RANK = 32
DIN = 8
CELLS = 2048
WIDTH = NZ * RANK
LOADS = 4
STEP = CELLS // LOADS
FAR = (4, 3, 5, 2, 6, 1, 7)
ROW, COL, PART, PROJ, SUM, LAT0, LAT1, RELAY = range(8)


def split3(value):
    high = value.astype(BF16).astype(F32)
    rest = value - high
    mid = rest.astype(BF16).astype(F32)
    return high, mid, rest - mid


def pick(index, *values):
    out = jnp.zeros(index.shape, F32)
    for place, value in enumerate(values):
        out = jnp.where(index == place, value, out)
    return out


def kernel(
    x_hbm, amp_hbm, len_hbm, noise_hbm, maps_hbm, basis_hbm, out_ref,
    x_ref, amp_ref, len_ref, noise_ref, maps, basis, basis_t, base, mine, rows_x, cols_x,
    part_wide, part, relay, part_in, proj, left, side, tile, sums, sums_in, lat_src, latent,
    load_sem, send_sem, recv_sem,
):
    run = lax.axis_index("runs")
    z = lax.axis_index("cells")
    y, x, core = run // (NX * NC), (run // NC) % NX, run % NC
    owner = core == 1
    early = z < HALF
    late = jnp.logical_not(early)

    def at(dy, dx, to, dz):
        place = ((y + dy + NY) % NY) * (NX * NC) + ((x + dx + NX) % NX) * NC + to
        return (place, (z + dz + NZ) % NZ)

    barrier = pltpu.get_barrier_semaphore()

    def greet(device):
        pl.semaphore_signal(barrier, inc=1, device_id=device, device_id_type=MESH)

    @pl.when(owner)
    def _():
        for d in FAR:
            greet(at(0, 0, 1, d))

            @pl.when(jnp.logical_or(early, (z + d) % NZ >= HALF))
            def _():
                greet(at(0, 0, 0, d))

    loads = []
    for c in range(LOADS):
        now = pl.ds(c * STEP, STEP)
        loads.append((
            pltpu.make_async_copy(maps_hbm.at[:, now], maps.at[:, now], load_sem.at[0, c]),
            pltpu.make_async_copy(basis_hbm.at[now], basis.at[now], load_sem.at[1, c]),
        ))
    small = [
        pltpu.make_async_copy(source, target, load_sem.at[2, place])
        for place, (source, target) in enumerate(
            ((x_hbm, x_ref), (len_hbm, len_ref), (amp_hbm, amp_ref), (noise_hbm, noise_ref))
        )
    ]
    for load in (*loads[0], *loads[1], *loads[2], *loads[3], *small):
        load.start()

    @pl.when(owner)
    def _():
        for d in FAR:
            for to in range(NC):
                greet(at(d, 0, to, 0))
        for d in (2, 1, 3):
            for to in range(NC):
                greet(at(0, d, to, 0))
        greet(at(0, 0, 0, 0))

    def remote(phase, source, target, device, away=None):
        return pltpu.make_async_remote_copy(
            src_ref=source, dst_ref=target, send_sem=send_sem.at[phase if away is None else away],
            recv_sem=recv_sem.at[phase], device_id=device, device_id_type=MESH,
        )

    def received(phase, target):
        remote(phase, target, target, at(0, 0, 1, 1)).wait_recv()

    def left_here(phase, source):
        remote(phase, source, source, at(0, 0, 1, 1)).wait_send()

    def send_row(d):
        remote(ROW, mine, rows_x.at[d * NC + core], at(d, 0, 1, 0)).start()

    def send_part(q):
        slot = (q - z + NZ) % NZ
        remote(PART, part.at[q], part_in.at[slot * NC + core], at(0, 0, 1, q - z)).start()

    def send_parts(first, last):
        for q in range(first, last):
            @pl.when(jnp.logical_or(core == 0, z != q))
            def _():
                send_part(q)

    total = jnp.zeros((ROWS, WIDTH), F32)
    for c in range(LOADS):
        for load in loads[c]:
            load.wait()
        now = pl.ds(c * STEP, STEP)
        total = total + jnp.dot(maps[:, now], basis[now, :], preferred_element_type=F32)
    turned = total.T.reshape(NZ, RANK, ROWS)
    part_wide[...] = turned
    part[...] = turned.astype(BF16)
    for load in small:
        load.wait()
    mine[...] = x_ref[...].astype(F32)

    @pl.when(jnp.logical_not(owner))
    def _():
        @pl.when(early)
        def _():
            pl.semaphore_wait(barrier, 14)
            remote(RELAY, part.at[pl.ds(HALF, HALF)], relay.at[:, 0], at(0, 0, 1, 0)).start()

        @pl.when(late)
        def _():
            pl.semaphore_wait(barrier, 18)

        send_row(0)

    @pl.when(owner)
    def _():
        @pl.when(early)
        def _():
            relay[:, 1] = part[HALF:]
            received(RELAY, part.at[pl.ds(0, HALF)])

        pl.semaphore_wait(barrier, 17)

        @pl.when(early)
        def _():
            for q in range(HALF, NZ):
                slot = (q - z + NZ) % NZ
                place = part_in.at[pl.ds(slot * NC, NC)]
                remote(PART, relay.at[q - HALF], place, at(0, 0, 1, q - z), RELAY).start()

    @pl.when(late)
    def _():
        send_parts(HALF, NZ)

    send_parts(0, HALF)
    for d in FAR:
        send_row(d)
    for d in (2, 1, 3):
        remote(COL, mine, cols_x.at[d * NC + core], at(0, d, 1, 0)).start()

    whole = (ROWS, ROWS)
    eye = lax.broadcasted_iota(jnp.int32, whole, 0) == lax.broadcasted_iota(jnp.int32, whole, 1)
    spread = jnp.where(eye, jnp.broadcast_to(noise_ref[...], whole), 0.0)
    noise = jnp.sum(spread, axis=1, keepdims=True)

    @pl.loop(0, CELLS // PAIR)
    def _(c):
        now = pl.ds(pl.multiple_of(c * PAIR, PAIR), PAIR)
        base[:, now] = noise * maps[:, now].astype(F32)
        basis_t[:, now] = basis[now, :].T

    @pl.when(owner)
    def _():
        length = len_ref[pl.ds(z, 1), :]
        square = (DIN, DIN)
        eye = lax.broadcasted_iota(jnp.int32, square, 0) == lax.broadcasted_iota(jnp.int32, square, 1)
        column = jnp.sum(jnp.where(eye, jnp.broadcast_to(length, square), 0.0), axis=1, keepdims=True)
        inverse = 1.0 / column
        squared = inverse * inverse
        lanes = lax.broadcasted_iota(jnp.int32, (1, NZ), 1)
        amp = jnp.sum(jnp.where(lanes == z, amp_ref[...], 0.0), axis=1, keepdims=True)

        def halves(inputs):
            scaled = inputs * inverse
            return split3(0.5 * jnp.sum(scaled * scaled, axis=0, keepdims=True))

        def side_by_side(ref, count):
            return jnp.concatenate([ref[k] for k in range(count)], 1)

        def place(count):
            return lax.broadcasted_iota(jnp.int32, (DIN, count), 0)

        received(PART, part_in.at[pl.ds(0, NZ * NC - 1)])
        own = [part_in[0].astype(F32), part_wide[z]]
        for d in range(1, NZ):
            for to in range(NC):
                own[to] = own[to] + part_in[d * NC + to].astype(F32)
        for to in range(NC):
            proj[0, to] = own[to].astype(BF16)
        for d in (2, 1, 3):
            remote(PROJ, proj.at[0], proj.at[d], at(0, d, 1, 0)).start()

        received(ROW, rows_x.at[pl.ds(0, NY * NC - 1)])
        rows_x[1] = mine[...]
        inputs = side_by_side(rows_x, NY * NC)
        ha, hb, hc = halves(inputs)
        wa, wb, wc = split3(inputs * squared)
        tail = pick(place(NY * PAIR), -ha, -hb, -hc, -1.0, -1.0, -1.0)
        side[...] = jnp.concatenate([wa, wb, wc, tail], 0).astype(BF16)
        received(COL, cols_x.at[pl.ds(0, (NX - 1) * NC)])
        for to in range(NC):
            cols_x[to] = rows_x[to]
        inputs = side_by_side(cols_x, NX * NC)
        ha, hb, hc = halves(inputs)
        tail = pick(place(NX * PAIR), 1.0, 1.0, 1.0, ha, hb, hc)
        left[...] = jnp.concatenate([inputs, inputs, inputs, tail], 0).T.astype(BF16)

        @pl.loop(0, NX)
        def _(d):
            now = pl.ds(pl.multiple_of(d * PAIR, PAIR), PAIR)
            logit = jnp.dot(left[now, :], side[...], preferred_element_type=F32)
            tile[d] = (amp * jnp.exp(jnp.minimum(logit, 0.0))).astype(BF16)

        received(PROJ, proj.at[pl.ds(1, NX - 1)])
        blocks = [jnp.concatenate([proj[d, 0], proj[d, 1]], 1) for d in range(NX)]
        def product(slot):
            now = pl.ds(pl.multiple_of(slot * PAIR, PAIR), PAIR)
            values = jnp.zeros((RANK, PAIR), F32)
            for e in range(NX):
                values = values + jnp.dot(blocks[e], tile[e, :, now], preferred_element_type=F32)
            return values

        for step in range(NY - 1):
            to_y = step + (step >= y).astype(jnp.int32)
            slot = (y - to_y + NY) % NY
            values = product(slot)
            sums[slot, 0] = values[:, :ROWS].astype(BF16)
            sums[slot, 1] = values[:, ROWS:].astype(BF16)
            remote(SUM, sums.at[slot], sums_in.at[slot], at(to_y - y, 0, 1, 0)).start()
        values = product(0)
        received(SUM, sums_in.at[pl.ds(1, NY - 1)])
        final = [values[:, :ROWS], values[:, ROWS:]]
        for d in range(1, NY):
            for to in range(NC):
                final[to] = final[to] + sums_in[d, to].astype(F32)
        for to in range(NC):
            lat_src[to] = final[to].astype(BF16)
        remote(LAT0, lat_src.at[0], latent.at[z], at(0, 0, 0, 0)).start()
        for step in range(NZ - 1):
            away = step + (step >= z).astype(jnp.int32) - z
            remote(LAT1, lat_src.at[1], latent.at[z], at(0, 0, 1, away)).start()
            remote(LAT0, lat_src.at[0], latent.at[z], at(0, 0, 0, away)).start()
        latent[z] = lat_src[1]

        left_here(ROW, rows_x.at[pl.ds(0, NY - 1)])
        left_here(COL, cols_x.at[pl.ds(0, NX - 1)])
        @pl.when(early)
        def _():
            left_here(PART, part.at[pl.ds(0, HALF - 1)])
            left_here(RELAY, part)

        @pl.when(late)
        def _():
            left_here(PART, part.at[pl.ds(0, NZ - 1)])

        left_here(PROJ, proj.at[pl.ds(0, NX - 1)])
        left_here(SUM, sums.at[pl.ds(0, NY - 1)])
        left_here(LAT0, part)
        left_here(LAT1, part.at[pl.ds(0, NZ - 1)])
        received(LAT1, latent.at[pl.ds(0, NZ - 1)])

    @pl.when(jnp.logical_not(owner))
    def _():
        left_here(ROW, rows_x.at[pl.ds(0, NY)])
        left_here(COL, cols_x.at[pl.ds(0, NX - 1)])
        @pl.when(early)
        def _():
            left_here(PART, part.at[pl.ds(0, HALF)])
            left_here(RELAY, part.at[pl.ds(0, HALF)])

        @pl.when(late)
        def _():
            left_here(PART, part)

        received(LAT0, latent)

    mixed = latent[...].reshape(WIDTH, ROWS).astype(F32).T.astype(BF16)
    for c in range(LOADS):
        now = pl.ds(c * STEP, STEP)
        expand = jnp.dot(mixed, basis_t[:, now], preferred_element_type=F32)
        out_ref[:, now] = (expand + base[:, now]).astype(BF16)


def shards(maps, run_inputs, basis, amplitude, length, noise):
    operands = (run_inputs, amplitude.reshape(1, NZ), length, noise.reshape(1, ROWS), maps, basis)
    operands = [pltpu.with_memory_space_constraint(a, pltpu.HBM) for a in operands]
    hbm = pl.BlockSpec(memory_space=pltpu.HBM)
    return pl.pallas_call(
        kernel,
        out_shape=pltpu.VMEM((ROWS, CELLS), BF16),
        in_specs=[hbm] * 6,
        out_specs=pl.BlockSpec(memory_space=pltpu.VMEM),
        scratch_shapes=[
            pltpu.VMEM((DIN, ROWS), BF16),
            pltpu.VMEM((1, NZ), F32),
            pltpu.VMEM((NZ, DIN), F32),
            pltpu.VMEM((1, ROWS), F32),
            pltpu.VMEM((ROWS, CELLS), BF16),
            pltpu.VMEM((CELLS, WIDTH), BF16),
            pltpu.VMEM((WIDTH, CELLS), BF16),
            pltpu.VMEM((ROWS, CELLS), F32),
            pltpu.VMEM((DIN, ROWS), F32),
            pltpu.VMEM((NY * NC, DIN, ROWS), F32),
            pltpu.VMEM((NX * NC, DIN, ROWS), F32),
            pltpu.VMEM((NZ, RANK, ROWS), F32),
            pltpu.VMEM((NZ, RANK, ROWS), BF16),
            pltpu.VMEM((HALF, NC, RANK, ROWS), BF16),
            pltpu.VMEM((NZ * NC, RANK, ROWS), BF16),
            pltpu.VMEM((NX, NC, RANK, ROWS), BF16),
            pltpu.VMEM((NX * PAIR, RANK), BF16),
            pltpu.VMEM((RANK, NY * PAIR), BF16),
            pltpu.VMEM((NX, PAIR, NY * PAIR), BF16),
            pltpu.VMEM((NY, NC, RANK, ROWS), BF16),
            pltpu.VMEM((NY, NC, RANK, ROWS), BF16),
            pltpu.VMEM((NC, RANK, ROWS), BF16),
            pltpu.VMEM((NZ, RANK, ROWS), BF16),
            pltpu.SemaphoreType.DMA((3, LOADS)),
            pltpu.SemaphoreType.DMA((8,)),
            pltpu.SemaphoreType.DMA((8,)),
        ],
        compiler_params=pltpu.CompilerParams(
            collective_id=0, has_side_effects=True, vmem_limit_bytes=32 * 1024 * 1024
        ),
    )(*operands)


def solution(mesh):
    in_specs = (P("runs", "cells"), P(None, "runs"), P("cells", None), P(), P(), P("runs"))
    out_specs = P("runs", "cells")
    return jax.shard_map(shards, mesh=mesh, in_specs=in_specs, out_specs=out_specs, check_vma=False)
```

```python
import jax
import jax.numpy as jnp
from jax import lax
from jax.experimental import pallas as pl
from jax.experimental.pallas import tpu as pltpu
from jax.sharding import PartitionSpec as P

MESH = pl.DeviceIdType.MESH
F32 = jnp.float32
BF16 = jnp.bfloat16
NY, NX, NC, NZ = 8, 4, 2, 8
ROWS = 128
OWNERS = 4
EACH = NZ // OWNERS
PAIR = NC * ROWS
RANK = 32
DIN = 8
CELLS = 2048
WIDTH = NZ * RANK
LOADS = 2
STEP = CELLS // LOADS
FAR = (4, 3, 5, 2, 6, 1, 7)
ROW, COL, PART, PROJ, SUM, LAT0, LAT1 = range(7)


def split3(value):
    high = value.astype(BF16).astype(F32)
    rest = value - high
    mid = rest.astype(BF16).astype(F32)
    return high, mid, rest - mid


def pick(index, *values):
    out = jnp.zeros(index.shape, F32)
    for place, value in enumerate(values):
        out = jnp.where(index == place, value, out)
    return out


def kernel(
    x_hbm, amp_hbm, len_hbm, noise_hbm, maps_hbm, basis_hbm, out_ref,
    x_ref, amp_ref, len_ref, noise_ref, maps, basis, basis_t, base, mine, rows_x, cols_x,
    part_wide, part, part_in, proj, left, side, tile, sums, sums_in, lat_src, latent,
    load_sem, send_sem, recv_sem,
):
    run = lax.axis_index("runs")
    z = lax.axis_index("cells")
    y, x, core = run // (NX * NC), (run // NC) % NX, run % NC
    early = z < OWNERS
    late = jnp.logical_not(early)
    owner = jnp.logical_and(core == 1, early)

    first = z * EACH

    def at(dy, dx, to, dz):
        place = ((y + dy + NY) % NY) * (NX * NC) + ((x + dx + NX) % NX) * NC + to
        return (place, (z + dz + NZ) % NZ)

    barrier = pltpu.get_barrier_semaphore()

    def greet(device):
        pl.semaphore_signal(barrier, inc=1, device_id=device, device_id_type=MESH)

    loads = []
    for c in range(LOADS):
        now = pl.ds(c * STEP, STEP)
        loads.append((
            pltpu.make_async_copy(maps_hbm.at[:, now], maps.at[:, now], load_sem.at[0, c]),
            pltpu.make_async_copy(basis_hbm.at[now], basis.at[now], load_sem.at[1, c]),
        ))
    small = [
        pltpu.make_async_copy(source, target, load_sem.at[2, place])
        for place, (source, target) in enumerate(
            ((x_hbm, x_ref), (len_hbm, len_ref), (amp_hbm, amp_ref), (noise_hbm, noise_ref))
        )
    ]
    for load in (*loads[0], *loads[1], *small):
        load.start()

    @pl.when(owner)
    def _():
        for d in FAR:
            for to in range(NC):
                greet(at(d, 0, to, 0))
        for d in (2, 1, 3):
            for to in range(NC):
                greet(at(0, d, to, 0))
        greet(at(0, 0, 0, 0))
        for d in FAR:
            for to in range(NC):
                greet(at(0, 0, to, d))

    def remote(phase, source, target, device):
        return pltpu.make_async_remote_copy(
            src_ref=source, dst_ref=target, send_sem=send_sem.at[phase],
            recv_sem=recv_sem.at[phase], device_id=device, device_id_type=MESH,
        )

    def received(phase, target):
        remote(phase, target, target, at(0, 0, 1, 1)).wait_recv()

    def left_here(phase, source):
        remote(phase, source, source, at(0, 0, 1, 1)).wait_send()

    def send_row(d):
        remote(ROW, mine, rows_x.at[d * NC + core], at(d, 0, 1, 0)).start()

    total = jnp.zeros((ROWS, WIDTH), F32)
    for c in range(LOADS):
        for load in loads[c]:
            load.wait()
        now = pl.ds(c * STEP, STEP)
        total = total + jnp.dot(maps[:, now], basis[now, :], preferred_element_type=F32)
    turned = total.T.reshape(NZ, RANK, ROWS)
    part_wide[...] = turned
    part[...] = turned.astype(BF16)

    @pl.when(late)
    def _():
        pl.semaphore_wait(barrier, OWNERS)

    @pl.when(jnp.logical_and(early, core == 0))
    def _():
        pl.semaphore_wait(barrier, OWNERS + NY + NX - 2)

    @pl.when(owner)
    def _():
        pl.semaphore_wait(barrier, OWNERS + NY + NX - 3)

    for step in range(OWNERS):
        plane = 3 - step

        @pl.when(jnp.logical_or(core == 0, z != plane))
        def _():
            slot = ((plane - z + NZ) % NZ) * NC + core
            source = part.at[pl.ds(plane * EACH, EACH)]
            remote(PART, source, part_in.at[slot], at(0, 0, 1, plane - z)).start()

    for load in small:
        load.wait()

    @pl.when(early)
    def _():
        mine[...] = x_ref[...].astype(F32)
        for d in FAR:
            send_row(d)
        for d in (2, 1, 3):
            remote(COL, mine, cols_x.at[d * NC + core], at(0, d, 1, 0)).start()

        @pl.when(core == 0)
        def _():
            send_row(0)

    whole = (ROWS, ROWS)
    eye = lax.broadcasted_iota(jnp.int32, whole, 0) == lax.broadcasted_iota(jnp.int32, whole, 1)
    spread = jnp.where(eye, jnp.broadcast_to(noise_ref[...], whole), 0.0)
    noise = jnp.sum(spread, axis=1, keepdims=True)

    @pl.loop(0, CELLS // PAIR)
    def _(c):
        now = pl.ds(pl.multiple_of(c * PAIR, PAIR), PAIR)
        base[:, now] = noise * maps[:, now].astype(F32)
        basis_t[:, now] = basis[now, :].T

    def side_by_side(ref, count):
        return jnp.concatenate([ref[k] for k in range(count)], 1)

    def place(count):
        return lax.broadcasted_iota(jnp.int32, (DIN, count), 0)

    def make_tile(slot):
        q = first + slot
        length = len_ref[pl.ds(q, 1), :]
        square = (DIN, DIN)
        eye = lax.broadcasted_iota(jnp.int32, square, 0) == lax.broadcasted_iota(jnp.int32, square, 1)
        column = jnp.sum(jnp.where(eye, jnp.broadcast_to(length, square), 0.0), axis=1, keepdims=True)
        inverse = 1.0 / column
        squared = inverse * inverse
        lanes = lax.broadcasted_iota(jnp.int32, (1, NZ), 1)
        amp = jnp.sum(jnp.where(lanes == q, amp_ref[...], 0.0), axis=1, keepdims=True)

        def halves(inputs):
            scaled = inputs * inverse
            return split3(0.5 * jnp.sum(scaled * scaled, axis=0, keepdims=True))

        inputs = side_by_side(rows_x, NY * NC)
        ha, hb, hc = halves(inputs)
        wa, wb, wc = split3(inputs * squared)
        last = pick(place(NY * PAIR), -ha, -hb, -hc, -1.0, -1.0, -1.0)
        side[...] = jnp.concatenate([wa, wb, wc, last], 0).astype(BF16)
        inputs = side_by_side(cols_x, NX * NC)
        ha, hb, hc = halves(inputs)
        last = pick(place(NX * PAIR), 1.0, 1.0, 1.0, ha, hb, hc)
        left[...] = jnp.concatenate([inputs, inputs, inputs, last], 0).T.astype(BF16)

        @pl.loop(0, NX)
        def _(d):
            now = pl.ds(pl.multiple_of(d * PAIR, PAIR), PAIR)
            logit = jnp.dot(left[now, :], side[...], preferred_element_type=F32)
            tile[slot, d] = (amp * jnp.exp(jnp.minimum(logit, 0.0))).astype(BF16)

    @pl.when(owner)
    def _():
        received(ROW, rows_x.at[pl.ds(0, NY * NC - 1)])
        rows_x[1] = mine[...]
        received(COL, cols_x.at[pl.ds(0, (NX - 1) * NC)])
        for to in range(NC):
            cols_x[to] = rows_x[to]
        make_tile(0)

        received(PART, part_in.at[pl.ds(0, NZ * NC - 1)])
        for slot in range(EACH):
            own = [part_in[0, slot].astype(F32), part_wide[first + slot]]
            for d in range(1, NZ):
                for to in range(NC):
                    own[to] = own[to] + part_in[d * NC + to, slot].astype(F32)
            for to in range(NC):
                proj[0, slot, to] = own[to].astype(BF16)
        for d in (2, 1, 3):
            remote(PROJ, proj.at[0], proj.at[d], at(0, d, 1, 0)).start()
        for slot in range(1, EACH):
            make_tile(slot)

        def product(row, slot):
            now = pl.ds(pl.multiple_of(row * PAIR, PAIR), PAIR)
            values = jnp.zeros((RANK, PAIR), F32)
            for e in range(NX):
                block = jnp.concatenate([proj[e, slot, 0], proj[e, slot, 1]], 1)
                values = values + jnp.dot(block, tile[slot, e, :, now], preferred_element_type=F32)
            return values

        received(PROJ, proj.at[pl.ds(1, NX - 1)])

        for step in range(NY - 1):
            to_y = step + (step >= y).astype(jnp.int32)
            row = (y - to_y + NY) % NY
            for slot in range(EACH):
                values = product(row, slot)
                for to in range(NC):
                    sums[row, slot, to] = values[:, to * ROWS:(to + 1) * ROWS].astype(BF16)
            remote(SUM, sums.at[row], sums_in.at[row], at(to_y - y, 0, 1, 0)).start()
        own = [product(0, slot) for slot in range(EACH)]
        received(SUM, sums_in.at[pl.ds(1, NY - 1)])
        for slot in range(EACH):
            for to in range(NC):
                final = own[slot][:, to * ROWS:(to + 1) * ROWS]
                for d in range(1, NY):
                    final = final + sums_in[d, slot, to].astype(F32)
                lat_src[to, slot] = final.astype(BF16)
        spot = latent.at[pl.ds(first, EACH)]
        remote(LAT0, lat_src.at[0], spot, at(0, 0, 0, 0)).start()
        for step in range(NZ - 1):
            away = step + (step >= z).astype(jnp.int32) - z
            remote(LAT1, lat_src.at[1], spot, at(0, 0, 1, away)).start()
            remote(LAT0, lat_src.at[0], spot, at(0, 0, 0, away)).start()
        for slot in range(EACH):
            latent[first + slot] = lat_src[1, slot]

        left_here(ROW, rows_x.at[pl.ds(0, NY - 1)])
        left_here(COL, cols_x.at[pl.ds(0, NX - 1)])
        left_here(PART, part.at[pl.ds(0, NZ - EACH)])
        left_here(PROJ, proj.at[pl.ds(1, NX - 1)])
        left_here(SUM, sums.at[pl.ds(0, NY - 1)])
        left_here(LAT0, part_in.at[pl.ds(0, NZ)])
        left_here(LAT1, part_in.at[pl.ds(0, NZ - 1)])
        received(LAT1, latent.at[pl.ds(0, NZ - EACH)])

    @pl.when(jnp.logical_not(owner))
    def _():
        left_here(PART, part)

        @pl.when(early)
        def _():
            left_here(ROW, rows_x.at[pl.ds(0, NY)])
            left_here(COL, cols_x.at[pl.ds(0, NX - 1)])

        @pl.when(core == 0)
        def _():
            received(LAT0, latent)

        @pl.when(core == 1)
        def _():
            received(LAT1, latent)

    mixed = latent[...].reshape(WIDTH, ROWS).astype(F32).T.astype(BF16)
    for c in range(LOADS):
        now = pl.ds(c * STEP, STEP)
        expand = jnp.dot(mixed, basis_t[:, now], preferred_element_type=F32)
        out_ref[:, now] = (expand + base[:, now]).astype(BF16)


def shards(maps, run_inputs, basis, amplitude, length, noise):
    operands = (run_inputs, amplitude.reshape(1, NZ), length, noise.reshape(1, ROWS), maps, basis)
    operands = [pltpu.with_memory_space_constraint(a, pltpu.HBM) for a in operands]
    hbm = pl.BlockSpec(memory_space=pltpu.HBM)
    return pl.pallas_call(
        kernel,
        out_shape=pltpu.VMEM((ROWS, CELLS), BF16),
        in_specs=[hbm] * 6,
        out_specs=pl.BlockSpec(memory_space=pltpu.VMEM),
        scratch_shapes=[
            pltpu.VMEM((DIN, ROWS), BF16),
            pltpu.VMEM((1, NZ), F32),
            pltpu.VMEM((NZ, DIN), F32),
            pltpu.VMEM((1, ROWS), F32),
            pltpu.VMEM((ROWS, CELLS), BF16),
            pltpu.VMEM((CELLS, WIDTH), BF16),
            pltpu.VMEM((WIDTH, CELLS), BF16),
            pltpu.VMEM((ROWS, CELLS), F32),
            pltpu.VMEM((DIN, ROWS), F32),
            pltpu.VMEM((NY * NC, DIN, ROWS), F32),
            pltpu.VMEM((NX * NC, DIN, ROWS), F32),
            pltpu.VMEM((NZ, RANK, ROWS), F32),
            pltpu.VMEM((NZ, RANK, ROWS), BF16),
            pltpu.VMEM((NZ * NC, EACH, RANK, ROWS), BF16),
            pltpu.VMEM((NX, EACH, NC, RANK, ROWS), BF16),
            pltpu.VMEM((NX * PAIR, RANK), BF16),
            pltpu.VMEM((RANK, NY * PAIR), BF16),
            pltpu.VMEM((EACH, NX, PAIR, NY * PAIR), BF16),
            pltpu.VMEM((NY, EACH, NC, RANK, ROWS), BF16),
            pltpu.VMEM((NY, EACH, NC, RANK, ROWS), BF16),
            pltpu.VMEM((NC, EACH, RANK, ROWS), BF16),
            pltpu.VMEM((NZ, RANK, ROWS), BF16),
            pltpu.SemaphoreType.DMA((3, 4)),
            pltpu.SemaphoreType.DMA((7,)),
            pltpu.SemaphoreType.DMA((7,)),
        ],
        compiler_params=pltpu.CompilerParams(
            collective_id=0, has_side_effects=True, vmem_limit_bytes=32 * 1024 * 1024
        ),
    )(*operands)


def solution(mesh):
    in_specs = (P("runs", "cells"), P(None, "runs"), P("cells", None), P(), P(), P("runs"))
    out_specs = P("runs", "cells")
    return jax.shard_map(shards, mesh=mesh, in_specs=in_specs, out_specs=out_specs, check_vma=False)
```

```python
import jax
import jax.numpy as jnp
from jax import lax
from jax.experimental import pallas as pl
from jax.experimental.pallas import tpu as pltpu
from jax.sharding import PartitionSpec as P

MESH = pl.DeviceIdType.MESH
F32 = jnp.float32
BF16 = jnp.bfloat16
NY, NX, NC, NZ = 8, 4, 2, 8
ROWS = 128
OWNERS = 4
EACH = NZ // OWNERS
PAIR = NC * ROWS
RANK = 32
DIN = 8
CELLS = 2048
WIDTH = NZ * RANK
LOADS = 2
STEP = CELLS // LOADS
FAR = (4, 3, 5, 2, 6, 1, 7)
TURN = (0, 1, 2, 7, 3, 6, 5, 4)
ROW, COL, PART, PART_LATE, PROJ, SUM, LAT0, LAT1 = range(8)


def split3(value):
    high = value.astype(BF16).astype(F32)
    rest = value - high
    mid = rest.astype(BF16).astype(F32)
    return high, mid, rest - mid


def pick(index, *values):
    out = jnp.zeros(index.shape, F32)
    for place, value in enumerate(values):
        out = jnp.where(index == place, value, out)
    return out


def kernel(
    x_hbm, amp_hbm, len_hbm, noise_hbm, maps_hbm, basis_hbm, out_ref,
    x_ref, amp_ref, len_ref, noise_ref, maps, basis, basis_t, base, mine, rows_x, cols_x,
    part, part_in, proj, left, side, tile, sums, sums_in, lat_src, latent,
    load_sem, send_sem, recv_sem,
):
    run = lax.axis_index("runs")
    z = lax.axis_index("cells")
    y, x, core = run // (NX * NC), (run // NC) % NX, run % NC
    early = z < OWNERS
    late = jnp.logical_not(early)
    owner = jnp.logical_and(core == 1, early)

    first = z * EACH

    def at(dy, dx, to, dz):
        place = ((y + dy + NY) % NY) * (NX * NC) + ((x + dx + NX) % NX) * NC + to
        return (place, (z + dz + NZ) % NZ)

    barrier = pltpu.get_barrier_semaphore()

    def greet(device):
        pl.semaphore_signal(barrier, inc=1, device_id=device, device_id_type=MESH)

    loads = []
    for c in range(LOADS):
        now = pl.ds(c * STEP, STEP)
        loads.append((
            pltpu.make_async_copy(maps_hbm.at[:, now], maps.at[:, now], load_sem.at[0, c]),
            pltpu.make_async_copy(basis_hbm.at[now], basis.at[now], load_sem.at[1, c]),
        ))
    small = [
        pltpu.make_async_copy(source, target, load_sem.at[2, place])
        for place, (source, target) in enumerate(
            ((x_hbm, x_ref), (len_hbm, len_ref), (amp_hbm, amp_ref), (noise_hbm, noise_ref))
        )
    ]
    for load in (*loads[0], *loads[1], *small):
        load.start()

    @pl.when(owner)
    def _():
        for d in FAR:
            for to in range(NC):
                greet(at(d, 0, to, 0))
        for d in (2, 1, 3):
            for to in range(NC):
                greet(at(0, d, to, 0))
        greet(at(0, 0, 0, 0))
        for d in FAR:
            for to in range(NC):
                greet(at(0, 0, to, d))

    def remote(phase, source, target, device, arrival=None):
        return pltpu.make_async_remote_copy(
            src_ref=source, dst_ref=target, send_sem=send_sem.at[phase],
            recv_sem=recv_sem.at[phase if arrival is None else arrival], device_id=device, device_id_type=MESH,
        )

    def received(phase, target):
        remote(phase, target, target, at(0, 0, 1, 1)).wait_recv()

    def left_here(phase, source):
        remote(phase, source, source, at(0, 0, 1, 1)).wait_send()

    def send_row(d):
        remote(ROW, mine, rows_x.at[d * NC + core], at(d, 0, 1, 0)).start()

    total = jnp.zeros((ROWS, WIDTH), F32)
    for c in range(LOADS):
        for load in loads[c]:
            load.wait()
        now = pl.ds(c * STEP, STEP)
        total = total + jnp.dot(maps[:, now], basis[now, :], preferred_element_type=F32)
    turned = total.T.reshape(NZ, RANK, ROWS)
    part[...] = turned.astype(BF16)

    @pl.when(late)
    def _():
        pl.semaphore_wait(barrier, OWNERS)

    @pl.when(jnp.logical_and(early, core == 0))
    def _():
        pl.semaphore_wait(barrier, OWNERS + NY + NX - 2)

    @pl.when(owner)
    def _():
        pl.semaphore_wait(barrier, OWNERS + NY + NX - 3)

    for plane in (2, 0, 3, 1):

        @pl.when(jnp.logical_or(core == 0, z != plane))
        def _():
            source = part.at[pl.ds(plane * EACH, EACH)]
            device = at(0, 0, 1, plane - z)
            remote(PART, source, part_in.at[z * NC + core], device, PART + late.astype(jnp.int32)).start()

    for load in small:
        load.wait()

    @pl.when(early)
    def _():
        mine[...] = x_ref[...].astype(F32)
        for d in FAR:
            send_row(d)
        for d in (2, 1, 3):
            remote(COL, mine, cols_x.at[d * NC + core], at(0, d, 1, 0)).start()

        @pl.when(core == 0)
        def _():
            send_row(0)

    whole = (ROWS, ROWS)
    eye = lax.broadcasted_iota(jnp.int32, whole, 0) == lax.broadcasted_iota(jnp.int32, whole, 1)
    spread = jnp.where(eye, jnp.broadcast_to(noise_ref[...], whole), 0.0)
    noise = jnp.sum(spread, axis=1, keepdims=True)

    @pl.loop(0, CELLS // PAIR)
    def _(c):
        now = pl.ds(pl.multiple_of(c * PAIR, PAIR), PAIR)
        base[:, now] = noise * maps[:, now].astype(F32)
        basis_t[:, now] = basis[now, :].T

    def side_by_side(ref, count):
        return jnp.concatenate([ref[k] for k in range(count)], 1)

    def place(count):
        return lax.broadcasted_iota(jnp.int32, (DIN, count), 0)

    def make_tile(slot):
        q = first + slot
        length = len_ref[pl.ds(q, 1), :]
        square = (DIN, DIN)
        eye = lax.broadcasted_iota(jnp.int32, square, 0) == lax.broadcasted_iota(jnp.int32, square, 1)
        column = jnp.sum(jnp.where(eye, jnp.broadcast_to(length, square), 0.0), axis=1, keepdims=True)
        inverse = 1.0 / column
        squared = inverse * inverse
        lanes = lax.broadcasted_iota(jnp.int32, (1, NZ), 1)
        amp = jnp.sum(jnp.where(lanes == q, amp_ref[...], 0.0), axis=1, keepdims=True)

        def halves(inputs):
            scaled = inputs * inverse
            return split3(0.5 * jnp.sum(scaled * scaled, axis=0, keepdims=True))

        inputs = side_by_side(rows_x, NY * NC)
        ha, hb, hc = halves(inputs)
        wa, wb, wc = split3(inputs * squared)
        last = pick(place(NY * PAIR), -ha, -hb, -hc, -1.0, -1.0, -1.0)
        side[...] = jnp.concatenate([wa, wb, wc, last], 0).astype(BF16)
        inputs = side_by_side(cols_x, NX * NC)
        ha, hb, hc = halves(inputs)
        last = pick(place(NX * PAIR), 1.0, 1.0, 1.0, ha, hb, hc)
        left[...] = jnp.concatenate([inputs, inputs, inputs, last], 0).T.astype(BF16)

        @pl.loop(0, NX)
        def _(d):
            now = pl.ds(pl.multiple_of(d * PAIR, PAIR), PAIR)
            logit = jnp.dot(left[now, :], side[...], preferred_element_type=F32)
            tile[slot, d] = (amp * jnp.exp(jnp.minimum(logit, 0.0))).astype(BF16)

    @pl.when(owner)
    def _():
        received(ROW, rows_x.at[pl.ds(0, NY * NC - 1)])
        rows_x[1] = mine[...]
        received(COL, cols_x.at[pl.ds(0, (NX - 1) * NC)])
        for to in range(NC):
            cols_x[to] = rows_x[to]
        make_tile(0)

        part_in[z * NC + 1] = part[pl.ds(first, EACH)]
        half = OWNERS * NC

        def add(total, begin):
            for k in range(begin, begin + half, NC):
                total = [
                    [total[slot][to] + part_in[k + to, slot].astype(F32) for to in range(NC)]
                    for slot in range(EACH)
                ]
            return total

        zero = [[jnp.zeros((RANK, ROWS), F32)] * NC] * EACH
        received(PART, part_in.at[pl.ds(0, half - 1)])
        own = add(zero, 0)
        received(PART_LATE, part_in.at[pl.ds(half, half)])
        own = add(own, half)
        for slot in range(EACH):
            for to in range(NC):
                proj[0, slot, to] = own[slot][to].astype(BF16)
        for d in (2, 1, 3):
            remote(PROJ, proj.at[0], proj.at[d], at(0, d, 1, 0)).start()
        for slot in range(1, EACH):
            make_tile(slot)

        def product(row, slot):
            now = pl.ds(pl.multiple_of(row * PAIR, PAIR), PAIR)
            values = jnp.zeros((RANK, PAIR), F32)
            for e in range(NX):
                block = jnp.concatenate([proj[e, slot, 0], proj[e, slot, 1]], 1)
                values = values + jnp.dot(block, tile[slot, e, :, now], preferred_element_type=F32)
            return values

        def look_up(values, index):
            found = jnp.int32(values[0])
            for k in range(1, len(values)):
                found = jnp.where(index == k, values[k], found)
            return found

        place_y = look_up([TURN.index(k) for k in range(NY)], y)
        turns = [look_up(TURN, step + (step >= place_y).astype(jnp.int32)) for step in range(NY - 1)]
        received(PROJ, proj.at[pl.ds(1, NX - 1)])

        for to_y in turns:
            row = (y - to_y + NY) % NY
            for slot in range(EACH):
                values = product(row, slot)
                for to in range(NC):
                    sums[row, slot, to] = values[:, to * ROWS:(to + 1) * ROWS].astype(BF16)
                remote(SUM, sums.at[row, slot], sums_in.at[row, slot], at(to_y - y, 0, 1, 0)).start()
        own = [product(0, slot) for slot in range(EACH)]
        left_here(ROW, rows_x.at[pl.ds(0, NY - 1)])
        left_here(COL, cols_x.at[pl.ds(0, NX - 1)])
        left_here(PART, part.at[pl.ds(0, NZ - EACH)])
        left_here(PROJ, proj.at[pl.ds(1, NX - 1)])
        left_here(SUM, sums.at[pl.ds(0, NY - 1)])
        received(SUM, sums_in.at[pl.ds(1, NY - 1)])
        for slot in range(EACH):
            for to in range(NC):
                final = own[slot][:, to * ROWS:(to + 1) * ROWS]
                for d in range(1, NY):
                    final = final + sums_in[d, slot, to].astype(F32)
                lat_src[to, slot] = final.astype(BF16)
        spot = latent.at[pl.ds(first, EACH)]
        remote(LAT0, lat_src.at[0], spot, at(0, 0, 0, 0)).start()
        for step in range(NZ - 1):
            away = step + (step >= z).astype(jnp.int32) - z
            remote(LAT1, lat_src.at[1], spot, at(0, 0, 1, away)).start()
            remote(LAT0, lat_src.at[0], spot, at(0, 0, 0, away)).start()
        for slot in range(EACH):
            latent[first + slot] = lat_src[1, slot]

        received(LAT1, latent.at[pl.ds(0, NZ - EACH)])

    @pl.when(jnp.logical_not(owner))
    def _():
        left_here(PART, part)

        @pl.when(early)
        def _():
            left_here(ROW, rows_x.at[pl.ds(0, NY)])
            left_here(COL, cols_x.at[pl.ds(0, NX - 1)])

        @pl.when(core == 0)
        def _():
            received(LAT0, latent)

        @pl.when(core == 1)
        def _():
            received(LAT1, latent)

    mixed = latent[...].reshape(WIDTH, ROWS).astype(F32).T.astype(BF16)
    for c in range(LOADS):
        now = pl.ds(c * STEP, STEP)
        expand = jnp.dot(mixed, basis_t[:, now], preferred_element_type=F32)
        out_ref[:, now] = (expand + base[:, now]).astype(BF16)

    @pl.when(owner)
    def _():
        left_here(LAT0, part_in.at[pl.ds(0, NZ)])
        left_here(LAT1, part_in.at[pl.ds(0, NZ - 1)])


def shards(maps, run_inputs, basis, amplitude, length, noise):
    operands = (run_inputs, amplitude.reshape(1, NZ), length, noise.reshape(1, ROWS), maps, basis)
    operands = [pltpu.with_memory_space_constraint(a, pltpu.HBM) for a in operands]
    hbm = pl.BlockSpec(memory_space=pltpu.HBM)
    return pl.pallas_call(
        kernel,
        out_shape=pltpu.VMEM((ROWS, CELLS), BF16),
        in_specs=[hbm] * 6,
        out_specs=pl.BlockSpec(memory_space=pltpu.VMEM),
        scratch_shapes=[
            pltpu.VMEM((DIN, ROWS), BF16),
            pltpu.VMEM((1, NZ), F32),
            pltpu.VMEM((NZ, DIN), F32),
            pltpu.VMEM((1, ROWS), F32),
            pltpu.VMEM((ROWS, CELLS), BF16),
            pltpu.VMEM((CELLS, WIDTH), BF16),
            pltpu.VMEM((WIDTH, CELLS), BF16),
            pltpu.VMEM((ROWS, CELLS), F32),
            pltpu.VMEM((DIN, ROWS), F32),
            pltpu.VMEM((NY * NC, DIN, ROWS), F32),
            pltpu.VMEM((NX * NC, DIN, ROWS), F32),
            pltpu.VMEM((NZ, RANK, ROWS), BF16),
            pltpu.VMEM((NZ * NC, EACH, RANK, ROWS), BF16),
            pltpu.VMEM((NX, EACH, NC, RANK, ROWS), BF16),
            pltpu.VMEM((NX * PAIR, RANK), BF16),
            pltpu.VMEM((RANK, NY * PAIR), BF16),
            pltpu.VMEM((EACH, NX, PAIR, NY * PAIR), BF16),
            pltpu.VMEM((NY, EACH, NC, RANK, ROWS), BF16),
            pltpu.VMEM((NY, EACH, NC, RANK, ROWS), BF16),
            pltpu.VMEM((NC, EACH, RANK, ROWS), BF16),
            pltpu.VMEM((NZ, RANK, ROWS), BF16),
            pltpu.SemaphoreType.DMA((3, 4)),
            pltpu.SemaphoreType.DMA((8,)),
            pltpu.SemaphoreType.DMA((8,)),
        ],
        compiler_params=pltpu.CompilerParams(
            collective_id=0, has_side_effects=True, vmem_limit_bytes=32 * 1024 * 1024
        ),
    )(*operands)


def solution(mesh):
    in_specs = (P("runs", "cells"), P(None, "runs"), P("cells", None), P(), P(), P("runs"))
    out_specs = P("runs", "cells")
    return jax.shard_map(shards, mesh=mesh, in_specs=in_specs, out_specs=out_specs, check_vma=False)
```

```python
import jax
import jax.numpy as jnp
from jax import lax
from jax.experimental import pallas as pl
from jax.experimental.pallas import tpu as pltpu
from jax.sharding import PartitionSpec as P

MESH = pl.DeviceIdType.MESH
F32 = jnp.float32
BF16 = jnp.bfloat16
NY, NX, NC, NZ = 8, 4, 2, 8
ROWS = 128
OWNERS = 4
EACH = NZ // OWNERS
PAIR = NC * ROWS
RANK = 32
DIN = 8
CELLS = 2048
WIDTH = NZ * RANK
LOADS = 2
STEP = CELLS // LOADS
FAR = (4, 3, 5, 2, 6, 1, 7)
TURN = (0, 1, 2, 7, 3, 6, 5, 4)
ROW, COL, PART, PART_LATE, PROJ, SUM, LAT0, LAT1 = range(8)


def split3(value):
    high = value.astype(BF16).astype(F32)
    rest = value - high
    mid = rest.astype(BF16).astype(F32)
    return high, mid, rest - mid


def pick(index, *values):
    out = jnp.zeros(index.shape, F32)
    for place, value in enumerate(values):
        out = jnp.where(index == place, value, out)
    return out


def kernel(
    x_hbm, amp_hbm, len_hbm, noise_hbm, maps_hbm, basis_hbm, out_ref,
    x_ref, amp_ref, len_ref, noise_ref, maps, basis, basis_t, base, mine, rows_x, cols_x,
    part, part_in, proj, left, side, tile, sums, sums_in, lat_src, latent,
    load_sem, send_sem, recv_sem,
):
    run = lax.axis_index("runs")
    z = lax.axis_index("cells")
    y, x, core = run // (NX * NC), (run // NC) % NX, run % NC
    early = z < OWNERS
    late = jnp.logical_not(early)
    owner = jnp.logical_and(core == 1, early)

    first = z * EACH

    def at(dy, dx, to, dz):
        place = ((y + dy + NY) % NY) * (NX * NC) + ((x + dx + NX) % NX) * NC + to
        return (place, (z + dz + NZ) % NZ)

    barrier = pltpu.get_barrier_semaphore()

    def greet(device):
        pl.semaphore_signal(barrier, inc=1, device_id=device, device_id_type=MESH)

    loads = []
    for c in range(LOADS):
        now = pl.ds(c * STEP, STEP)
        loads.append((
            pltpu.make_async_copy(maps_hbm.at[:, now], maps.at[:, now], load_sem.at[0, c]),
            pltpu.make_async_copy(basis_hbm.at[now], basis.at[now], load_sem.at[1, c]),
        ))
    small = [
        pltpu.make_async_copy(source, target, load_sem.at[2, place])
        for place, (source, target) in enumerate(
            ((x_hbm, x_ref), (len_hbm, len_ref), (amp_hbm, amp_ref), (noise_hbm, noise_ref))
        )
    ]
    for load in (*loads[0], *loads[1], *small):
        load.start()

    @pl.when(owner)
    def _():
        for d in FAR:
            for to in range(NC):
                greet(at(d, 0, to, 0))
        for d in (2, 1, 3):
            for to in range(NC):
                greet(at(0, d, to, 0))
        greet(at(0, 0, 0, 0))
        for d in FAR:
            for to in range(NC):
                greet(at(0, 0, to, d))

    def remote(phase, source, target, device, arrival=None):
        return pltpu.make_async_remote_copy(
            src_ref=source, dst_ref=target, send_sem=send_sem.at[phase],
            recv_sem=recv_sem.at[phase if arrival is None else arrival], device_id=device, device_id_type=MESH,
        )

    def received(phase, target):
        remote(phase, target, target, at(0, 0, 1, 1)).wait_recv()

    def left_here(phase, source):
        remote(phase, source, source, at(0, 0, 1, 1)).wait_send()

    def send_row(d):
        remote(ROW, mine, rows_x.at[d * NC + core], at(d, 0, 1, 0)).start()

    total = jnp.zeros((ROWS, WIDTH), F32)
    for c in range(LOADS):
        for load in loads[c]:
            load.wait()
        now = pl.ds(c * STEP, STEP)
        total = total + jnp.dot(maps[:, now], basis[now, :], preferred_element_type=F32)
    turned = total.T.reshape(NZ, RANK, ROWS)
    part[...] = turned.astype(BF16)

    @pl.when(late)
    def _():
        pl.semaphore_wait(barrier, OWNERS)

    @pl.when(jnp.logical_and(early, core == 0))
    def _():
        pl.semaphore_wait(barrier, OWNERS + NY + NX - 2)

    @pl.when(owner)
    def _():
        pl.semaphore_wait(barrier, OWNERS + NY + NX - 3)

    for plane in (2, 0, 3, 1):

        @pl.when(jnp.logical_or(core == 0, z != plane))
        def _():
            source = part.at[pl.ds(plane * EACH, EACH)]
            device = at(0, 0, 1, plane - z)
            remote(PART, source, part_in.at[z * NC + core], device, PART + late.astype(jnp.int32)).start()

    for load in small:
        load.wait()

    @pl.when(early)
    def _():
        mine[...] = x_ref[...].astype(F32)
        for d in FAR:
            send_row(d)
        for d in (2, 1, 3):
            remote(COL, mine, cols_x.at[d * NC + core], at(0, d, 1, 0)).start()

        @pl.when(core == 0)
        def _():
            send_row(0)

    whole = (ROWS, ROWS)
    eye = lax.broadcasted_iota(jnp.int32, whole, 0) == lax.broadcasted_iota(jnp.int32, whole, 1)
    spread = jnp.where(eye, jnp.broadcast_to(noise_ref[...], whole), 0.0)
    noise = jnp.sum(spread, axis=1, keepdims=True)

    @pl.loop(0, CELLS // PAIR)
    def _(c):
        now = pl.ds(pl.multiple_of(c * PAIR, PAIR), PAIR)
        base[:, now] = noise * maps[:, now].astype(F32)
        basis_t[:, now] = basis[now, :].T

    def side_by_side(ref, count):
        return jnp.concatenate([ref[k] for k in range(count)], 1)

    def place(count):
        return lax.broadcasted_iota(jnp.int32, (DIN, count), 0)

    def make_tile(slot):
        q = first + slot
        length = len_ref[pl.ds(q, 1), :]
        square = (DIN, DIN)
        eye = lax.broadcasted_iota(jnp.int32, square, 0) == lax.broadcasted_iota(jnp.int32, square, 1)
        column = jnp.sum(jnp.where(eye, jnp.broadcast_to(length, square), 0.0), axis=1, keepdims=True)
        inverse = 1.0 / column
        squared = inverse * inverse
        lanes = lax.broadcasted_iota(jnp.int32, (1, NZ), 1)
        amp = jnp.sum(jnp.where(lanes == q, amp_ref[...], 0.0), axis=1, keepdims=True)

        def halves(inputs):
            scaled = inputs * inverse
            return split3(0.5 * jnp.sum(scaled * scaled, axis=0, keepdims=True))

        inputs = side_by_side(rows_x, NY * NC)
        ha, hb, hc = halves(inputs)
        wa, wb, wc = split3(inputs * squared)
        last = pick(place(NY * PAIR), -ha, -hb, -hc, -1.0, -1.0, -1.0)
        side[...] = jnp.concatenate([wa, wb, wc, last], 0).astype(BF16)
        inputs = side_by_side(cols_x, NX * NC)
        ha, hb, hc = halves(inputs)
        last = pick(place(NX * PAIR), 1.0, 1.0, 1.0, ha, hb, hc)
        left[...] = jnp.concatenate([inputs, inputs, inputs, last], 0).T.astype(BF16)

        @pl.loop(0, NX)
        def _(d):
            now = pl.ds(pl.multiple_of(d * PAIR, PAIR), PAIR)
            logit = jnp.dot(left[now, :], side[...], preferred_element_type=F32)
            tile[slot, d] = (amp * jnp.exp(jnp.minimum(logit, 0.0))).astype(BF16)

    @pl.when(owner)
    def _():
        received(ROW, rows_x.at[pl.ds(0, NY * NC - 1)])
        rows_x[1] = mine[...]
        received(COL, cols_x.at[pl.ds(0, (NX - 1) * NC)])
        for to in range(NC):
            cols_x[to] = rows_x[to]
        make_tile(0)

        part_in[z * NC + 1] = part[pl.ds(first, EACH)]
        half = OWNERS * NC

        def add(total, begin):
            for k in range(begin, begin + half, NC):
                total = [
                    [total[slot][to] + part_in[k + to, slot].astype(F32) for to in range(NC)]
                    for slot in range(EACH)
                ]
            return total

        zero = [[jnp.zeros((RANK, ROWS), F32)] * NC] * EACH
        received(PART, part_in.at[pl.ds(0, half - 1)])
        own = add(zero, 0)
        received(PART_LATE, part_in.at[pl.ds(half, half)])
        own = add(own, half)
        for slot in range(EACH):
            for to in range(NC):
                proj[0, slot, to] = own[slot][to].astype(BF16)
        for d in (2, 1, 3):
            remote(PROJ, proj.at[0], proj.at[d], at(0, d, 1, 0)).start()
        for slot in range(1, EACH):
            make_tile(slot)

        def product(row, slot):
            now = pl.ds(pl.multiple_of(row * PAIR, PAIR), PAIR)
            values = jnp.zeros((RANK, PAIR), F32)
            for e in range(NX):
                block = jnp.concatenate([proj[e, slot, 0], proj[e, slot, 1]], 1)
                values = values + jnp.dot(block, tile[slot, e, :, now], preferred_element_type=F32)
            return values

        def look_up(values, index):
            found = jnp.int32(values[0])
            for k in range(1, len(values)):
                found = jnp.where(index == k, values[k], found)
            return found

        place_y = look_up([TURN.index(k) for k in range(NY)], y)
        turns = [look_up(TURN, step + (step >= place_y).astype(jnp.int32)) for step in range(NY - 1)]
        received(PROJ, proj.at[pl.ds(1, NX - 1)])

        for to_y in turns:
            row = (y - to_y + NY) % NY
            for slot in range(EACH):
                values = product(row, slot)
                for to in range(NC):
                    sums[row, slot, to] = values[:, to * ROWS:(to + 1) * ROWS].astype(BF16)
                remote(SUM, sums.at[row, slot], sums_in.at[row, slot], at(to_y - y, 0, 1, 0)).start()
        own = [product(0, slot) for slot in range(EACH)]
        left_here(ROW, rows_x.at[pl.ds(0, NY - 1)])
        left_here(COL, cols_x.at[pl.ds(0, NX - 1)])
        left_here(PART, part.at[pl.ds(0, NZ - EACH)])
        left_here(PROJ, proj.at[pl.ds(1, NX - 1)])
        left_here(SUM, sums.at[pl.ds(0, NY - 1)])
        received(SUM, sums_in.at[pl.ds(1, NY - 1)])
        for slot in range(EACH):
            for to in range(NC):
                final = own[slot][:, to * ROWS:(to + 1) * ROWS]
                for d in range(1, NY):
                    final = final + sums_in[d, slot, to].astype(F32)
                lat_src[to, slot] = final.astype(BF16)
        spot = latent.at[pl.ds(first, EACH)]
        remote(LAT0, lat_src.at[0], spot, at(0, 0, 0, 0)).start()
        for step in range(NZ - 1):
            away = step + (step >= z).astype(jnp.int32) - z
            remote(LAT1, lat_src.at[1], spot, at(0, 0, 1, away)).start()
            remote(LAT0, lat_src.at[0], spot, at(0, 0, 0, away)).start()
        for slot in range(EACH):
            latent[first + slot] = lat_src[1, slot]

        received(LAT1, latent.at[pl.ds(0, NZ - EACH)])

    @pl.when(jnp.logical_not(owner))
    def _():
        left_here(PART, part)

        @pl.when(early)
        def _():
            left_here(ROW, rows_x.at[pl.ds(0, NY)])
            left_here(COL, cols_x.at[pl.ds(0, NX - 1)])

        @pl.when(core == 0)
        def _():
            received(LAT0, latent)

        @pl.when(core == 1)
        def _():
            received(LAT1, latent)

    mixed = latent[...].reshape(WIDTH, ROWS).T
    for c in range(LOADS):
        now = pl.ds(c * STEP, STEP)
        expand = jnp.dot(mixed, basis_t[:, now], preferred_element_type=F32)
        out_ref[:, now] = (expand + base[:, now]).astype(BF16)

    @pl.when(owner)
    def _():
        left_here(LAT0, part_in.at[pl.ds(0, NZ)])
        left_here(LAT1, part_in.at[pl.ds(0, NZ - 1)])


def shards(maps, run_inputs, basis, amplitude, length, noise):
    operands = (run_inputs, amplitude.reshape(1, NZ), length, noise.reshape(1, ROWS), maps, basis)
    operands = [pltpu.with_memory_space_constraint(a, pltpu.HBM) for a in operands]
    hbm = pl.BlockSpec(memory_space=pltpu.HBM)
    return pl.pallas_call(
        kernel,
        out_shape=pltpu.VMEM((ROWS, CELLS), BF16),
        in_specs=[hbm] * 6,
        out_specs=pl.BlockSpec(memory_space=pltpu.VMEM),
        scratch_shapes=[
            pltpu.VMEM((DIN, ROWS), BF16),
            pltpu.VMEM((1, NZ), F32),
            pltpu.VMEM((NZ, DIN), F32),
            pltpu.VMEM((1, ROWS), F32),
            pltpu.VMEM((ROWS, CELLS), BF16),
            pltpu.VMEM((CELLS, WIDTH), BF16),
            pltpu.VMEM((WIDTH, CELLS), BF16),
            pltpu.VMEM((ROWS, CELLS), F32),
            pltpu.VMEM((DIN, ROWS), F32),
            pltpu.VMEM((NY * NC, DIN, ROWS), F32),
            pltpu.VMEM((NX * NC, DIN, ROWS), F32),
            pltpu.VMEM((NZ, RANK, ROWS), BF16),
            pltpu.VMEM((NZ * NC, EACH, RANK, ROWS), BF16),
            pltpu.VMEM((NX, EACH, NC, RANK, ROWS), BF16),
            pltpu.VMEM((NX * PAIR, RANK), BF16),
            pltpu.VMEM((RANK, NY * PAIR), BF16),
            pltpu.VMEM((EACH, NX, PAIR, NY * PAIR), BF16),
            pltpu.VMEM((NY, EACH, NC, RANK, ROWS), BF16),
            pltpu.VMEM((NY, EACH, NC, RANK, ROWS), BF16),
            pltpu.VMEM((NC, EACH, RANK, ROWS), BF16),
            pltpu.VMEM((NZ, RANK, ROWS), BF16),
            pltpu.SemaphoreType.DMA((3, 4)),
            pltpu.SemaphoreType.DMA((8,)),
            pltpu.SemaphoreType.DMA((8,)),
        ],
        compiler_params=pltpu.CompilerParams(
            collective_id=0, has_side_effects=True, vmem_limit_bytes=32 * 1024 * 1024
        ),
    )(*operands)


def solution(mesh):
    in_specs = (P("runs", "cells"), P(None, "runs"), P("cells", None), P(), P(), P("runs"))
    out_specs = P("runs", "cells")
    return jax.shard_map(shards, mesh=mesh, in_specs=in_specs, out_specs=out_specs, check_vma=False)
```
